32 devices in a mesh: dp: 4 (over z), expert: 8 (over y, x, core).
Axes of the slice: x: 2, y: 2, z: 4, core: 2. Of those that a mesh axis runs over, the one named last changes fastest.
Arguments:
- tokens: bfloat16 [16384, 1024], P(('dp', 'expert')), may hold values from -12 to 12
- lengths: int32 [32, 2], P(('dp', 'expert')), may hold values from 1 to 448, 512 in all within a row
- routes: int32 [16384, 2], P(('dp', 'expert')), may hold values from 0 to 7, all different within a row; in each aligned block of 512 rows (0 to 511, 512 to 1023, ...) at most 256 rows name the same one
- cotangent: bfloat16 [16384, 1024], P(('dp', 'expert')), may hold values from -6 to 6
- gain_attn: bfloat16 [1024], P('dp'), may hold values from 0.5 to 1.5
- w_query: bfloat16 [1024, 1024], P('dp'), may hold values from -0.1875 to 0.1875
- key_projection_weight: bfloat16 [1024, 512], P('dp'), may hold values from -0.1875 to 0.1875
- value_projection_weight: bfloat16 [1024, 512], P('dp'), may hold values from -0.1875 to 0.1875
- w_out: bfloat16 [1024, 1024], P('dp'), may hold values from -1 to 1
- gain_moe: bfloat16 [1024], P('dp'), may hold values from 0.5 to 1.5
- w_router: bfloat16 [1024, 8], P('dp'), may hold values from -0.09375 to 0.09375
- w_gate: bfloat16 [8, 1024, 512], P('expert'), may hold values from -0.1875 to 0.1875
- w_up: bfloat16 [8, 1024, 512], P('expert'), may hold values from -0.1875 to 0.1875
- w_down: bfloat16 [8, 512, 1024], P('expert'), may hold values from -0.75 to 0.75
Outputs:
- mixed: bfloat16 [16384, 1024], P(('dp', 'expert'))
- grad_tokens: bfloat16 [16384, 1024], P(('dp', 'expert'))
- grad_gain_attn: float32 [1024], P('dp')
- grad_query: float32 [1024, 1024], P('dp')
- key_matrix_gradient: float32 [1024, 512], P('dp')
- value_matrix_gradient: float32 [1024, 512], P('dp')
- grad_out: float32 [1024, 1024], P('dp')
- grad_gain_moe: float32 [1024], P('dp')
- grad_router: float32 [1024, 8], P('dp')
- grad_gate: float32 [8, 1024, 512], P('expert', 'dp')
- grad_up: float32 [8, 1024, 512], P('expert', 'dp')
- grad_down: float32 [8, 512, 1024], P('expert', 'dp')
The draws below stay inside these ranges and needn't reach their ends.
Inputs may be any that keep to these rules, and one draw needn't show every extreme that they name: In the 512 rows of one device no expert is named by more than 256 routes, a bound that some block reaches; a token's 2 experts differ. Each device's 2 lengths sum to 512; its longest is at most 448.
All inputs are finite; a program needn't handle non-finite values.
Results may differ from the reference program's by a relative error of at most 0.023.
Values may be sent and summed in bfloat16 or wider, within the bound.
No kernel may reach another device: no remote copies, remote signals or barrier semaphores. Data moves between devices by JAX's collectives and lax.ppermute only.
A program may use at most 256 MiB of HBM per device.

```python
import math
import jax
import jax.numpy as jnp
import numpy as np
from jax import lax

MODEL_DIMENSION = 1024
QUERY_HEADS = 16
KEY_VALUE_HEADS = 8
HEAD_DIMENSION = 64
FF = 512
TOK_DEV = 512
SEQS = 2
MOST = 448
EXPERTS = 8
TOP = 2
CAP = 256
TOKENS = 16384
DEVICES = 32


def strengthened(values, key, source, target, shards_of, factor):
    owner, partner = [(jnp.arange(values.shape[axis_at]) // (values.shape[axis_at] // shards_of)).reshape([-1 if axis == axis_at else 1 for axis in range(values.ndim)]) for axis_at in (source, target)]
    chosen = jax.random.permutation(key, shards_of)[partner]
    strong = (owner == chosen) | (owner == (partner + shards_of // 2) % shards_of)
    return jnp.where(strong, factor * values, values)


def levels(key, shape, shards, least, largest):
    factor_of = 1.0
    for position, blocks in shards:
        draws = jax.random.uniform(jax.random.fold_in(jax.random.fold_in(key, 6), position), (blocks,), jnp.float32, least / len(shards), largest / len(shards))
        factor_of = factor_of * jnp.repeat(jnp.exp(draws), shape[position] // blocks).reshape((-1,) + (1,) * (len(shape) - 1 - position))
    return factor_of


def split_up(number_of, total, limit, lean):
    loads = [(1 << 20) // math.isqrt(grade ** lean) + 1 for grade in range(2, number_of + 1)]
    spare, given = total - limit - (number_of - 1), [1] * (number_of - 1)
    while spare > 0:
        candidates = [i for i in range(number_of - 1) if given[i] < limit]
        mass, left = sum([loads[i] for i in candidates]), spare
        for i in candidates:
            more = min(limit - given[i], max(1, left * loads[i] // mass), spare)
            given[i] = given[i] + more
            spare = spare - more
    return np.array([limit] + given)


def ragged_sizes(stream_key, number_of, total, reach, slope):
    if number_of == 2:
        one = jax.random.randint(stream_key, (), max(1, total - reach), min(reach, total - 1) + 1)
        return jnp.stack([one, total - one])
    sizes = jnp.asarray(split_up(number_of, total, reach, slope), jnp.int32)
    twos = (number_of - 1) // 2
    donor, receiver = sizes[1:1 + 2 * twos:2], sizes[2:2 + 2 * twos:2]
    slack = jnp.minimum(donor - 1, reach - receiver)
    moved = jax.random.randint(jax.random.fold_in(stream_key, 1), (twos,), 0, 1 << 20) % (slack + 1)
    sizes = sizes.at[1:1 + 2 * twos:2].set(donor - moved).at[2:2 + 2 * twos:2].set(receiver + moved)
    return sizes[jax.random.permutation(jax.random.fold_in(stream_key, 2), number_of)]


def routed_block(stream_key, own, number, rows, amount, top, most, slope):
    order = jax.random.permutation(stream_key, amount)
    heavy_load, common = portions_of(amount, rows * top, most, slope, True), portions_of(amount, rows * top, most, slope, False)
    places = jnp.arange(amount)

    def named(sizes, rotation):
        used = int((sizes > 0).sum())
        fixed = max(1, used // 4)
        shifted = fixed + (places - fixed + rotation * (used - fixed)) % max(1, amount - fixed)
        return jnp.zeros((amount,), jnp.int32).at[order[jnp.where(places < fixed, places, shifted)]].set(jnp.asarray(sizes, jnp.int32))

    sizes = jnp.where(number % 4 == 0, named(heavy_load, number // 4), named(common, number - number // 4 - 1))
    mixed = jax.random.permutation(jax.random.fold_in(own, 3), amount)
    giver, receiver = mixed[0:amount // 2 * 2:2], mixed[1:amount // 2 * 2:2]
    margin = jnp.minimum(sizes[giver] - 1, most - sizes[receiver]) // 2
    margin = jnp.where((giver == order[0]) | (receiver == order[0]) | (sizes[receiver] == 0), 0, jnp.maximum(margin, 0))
    shifted = jax.random.randint(jax.random.fold_in(own, 4), (amount // 2,), 0, 1 << 20) % (margin + 1)
    sizes = sizes.at[giver].add(-shifted).at[receiver].add(shifted)
    items = jnp.searchsorted(jnp.cumsum(sizes), jnp.arange(rows * top), side="right").astype(jnp.int32)
    table = items.reshape(top, rows).T
    table = table[jax.random.permutation(jax.random.fold_in(own, 1), rows)]
    rotation = jax.random.randint(jax.random.fold_in(own, 2), (rows, 1), 0, top)
    return jnp.take_along_axis(table, (jnp.arange(top)[None, :] + rotation) % top, axis=1)


def portions_of(count, total, bound, lean, full):
    weights = [(1 << 20) // math.isqrt(rank ** lean) + 1 for rank in range(1, count + 1)]
    largest = bound if full else min(bound, max(-(-total // count), total * weights[0] // sum(weights)))
    least = 1 if total - largest >= count - 1 else 0
    holding, rest = [largest] + [least] * (count - 1), total - largest - least * (count - 1)
    while rest > 0:
        candidates = [i for i in range(1, count) if holding[i] < largest] or [i for i in range(1, count) if holding[i] < bound]
        pool, left = sum([weights[i] for i in candidates]), rest
        for i in candidates:
            extra = min(bound - holding[i], max(1, left * weights[i] // pool), rest)
            holding[i] = holding[i] + extra
            rest = rest - extra
    return np.array(holding)


def noise(stream_key, extent, deviation, reach, shards=(), held_as=jnp.bfloat16):
    loudness = levels(stream_key, extent, shards, -0.22, 0.18) if shards else 1.0
    values = jax.random.normal(stream_key, extent, jnp.float32) * deviation * loudness
    return jnp.minimum(jnp.maximum(values, -reach), reach).astype(held_as)


def noise_with(key, dims, scale, most, cuts, heavy, kind=jnp.bfloat16):
    values = scale * jax.random.normal(key, dims, jnp.float32)
    if cuts:
        values = values * levels(key, dims, cuts, -0.22, 0.18)
    return jnp.clip(strengthened(values, jax.random.fold_in(key, 3), *heavy), -most, most).astype(kind)


def setup_inputs(seed: int = 0) -> dict:
    arg_keys = jax.random.split(jax.random.key(seed), 15)
    tokens = noise_with(arg_keys[0], (TOKENS, MODEL_DIMENSION), 1.0, 12.0, ((0, 32),), (0, 1, 32, 2.75))
    lengths = jax.vmap(lambda own: ragged_sizes(own, SEQS, TOK_DEV, MOST, 2))(jax.random.split(arg_keys[1], DEVICES)).reshape((DEVICES, SEQS)).astype(jnp.int32)
    routes_keys = jax.random.split(jax.random.fold_in(arg_keys[2], 1), TOKENS // TOK_DEV)
    routes_turns = jax.random.permutation(jax.random.fold_in(arg_keys[2], 3), TOKENS // TOK_DEV)
    routes = jax.vmap(lambda own, number: routed_block(jax.random.fold_in(arg_keys[2], 2), own, number, TOK_DEV, EXPERTS, TOP, CAP, 2))(routes_keys, routes_turns).reshape((TOKENS, TOP))
    cotangent = noise(arg_keys[3], (TOKENS, MODEL_DIMENSION), 1.0, 6.0, ((0, 32),))
    gain_attn = jnp.clip(1.0 + 0.1 * jax.random.normal(arg_keys[4], (MODEL_DIMENSION,), jnp.float32), 0.5, 1.5).astype(jnp.bfloat16)
    w_query = noise(arg_keys[5], (MODEL_DIMENSION, QUERY_HEADS * HEAD_DIMENSION), MODEL_DIMENSION ** -0.5, 0.1875, ((0, 4),))
    key_projection_weight = noise(arg_keys[6], (MODEL_DIMENSION, KEY_VALUE_HEADS * HEAD_DIMENSION), MODEL_DIMENSION ** -0.5, 0.1875, ((0, 4),))
    value_projection_weight = noise(arg_keys[7], (MODEL_DIMENSION, KEY_VALUE_HEADS * HEAD_DIMENSION), MODEL_DIMENSION ** -0.5, 0.1875, ((0, 4),))
    w_out = noise(arg_keys[8], (QUERY_HEADS * HEAD_DIMENSION, MODEL_DIMENSION), (QUERY_HEADS * HEAD_DIMENSION // 32) ** -0.5, 1.0, ((0, 4),))
    gain_moe = jnp.clip(1.0 + 0.1 * jax.random.normal(arg_keys[9], (MODEL_DIMENSION,), jnp.float32), 0.5, 1.5).astype(jnp.bfloat16)
    w_router = noise(arg_keys[10], (MODEL_DIMENSION, EXPERTS), (0.5 * MODEL_DIMENSION ** -0.5), 0.09375, ((0, 4),))
    w_gate = noise(arg_keys[11], (EXPERTS, MODEL_DIMENSION, FF), MODEL_DIMENSION ** -0.5, 0.1875, ((0, 8),))
    w_up = noise(arg_keys[12], (EXPERTS, MODEL_DIMENSION, FF), MODEL_DIMENSION ** -0.5, 0.1875, ((0, 8),))
    w_down = noise(arg_keys[13], (EXPERTS, FF, MODEL_DIMENSION), (FF // 8) ** -0.5, 0.75, ((0, 8),))
    return dict(tokens=tokens, lengths=lengths, routes=routes, cotangent=cotangent, gain_attn=gain_attn, w_query=w_query, key_projection_weight=key_projection_weight, value_projection_weight=value_projection_weight, w_out=w_out, gain_moe=gain_moe, w_router=w_router, w_gate=w_gate, w_up=w_up, w_down=w_down)


eps_norm = 1e-06
highest = lax.Precision.HIGHEST

@jax.custom_vjp
def lower_precision(v):
    return lax.optimization_barrier(v.astype(jnp.bfloat16)).astype(jnp.float32)

@jax.custom_vjp
def lower_precision_backward(v):
    return v

def low_keep(v):
    return (lower_precision(v), None)

def low_pass(kept, grad):
    return (grad,)

def back_keep(v):
    return (v, None)

def back_low(kept, grad):
    return (lower_precision(grad),)
lower_precision.defvjp(low_keep, low_pass)
lower_precision_backward.defvjp(back_keep, back_low)

def matrix_product(left, right):
    return jnp.dot(left, right, precision=highest, preferred_element_type=jnp.float32)

def rms_scale(values, gain):
    return values * lax.rsqrt(lax.optimization_barrier(jnp.mean(values * values, axis=-1, keepdims=True)) + eps_norm) * gain

def positions_of(lengths_row, count_of_rows):
    index_rows = jnp.arange(count_of_rows, dtype=jnp.int32)
    ends = jnp.cumsum(lengths_row).astype(jnp.int32)
    member = lax.optimization_barrier(jnp.sum((index_rows[:, None] >= ends[None, :]).astype(jnp.int32), axis=1))
    starts = ends - lengths_row.astype(jnp.int32)
    onehot = member[:, None] == jnp.arange(lengths_row.shape[0], dtype=jnp.int32)[None, :]
    begin = lax.optimization_barrier(jnp.sum(jnp.where(onehot, starts[None, :], 0), axis=1))
    return (member, index_rows - begin)

def rope_tables(positions, head_size):
    half_size = head_size // 2
    freq = jnp.exp(jnp.arange(half_size, dtype=jnp.float32) * (-2.0 * math.log(10000.0) / head_size))
    angle = positions.astype(jnp.float32)[:, None] * freq[None, :]
    return (jnp.cos(angle), jnp.sin(angle))

def apply_rotary(values, cosine_table, sine_table):
    half_size = values.shape[-1] // 2
    first = values[..., :half_size]
    second = values[..., half_size:]
    cos_b = cosine_table[:, None, :]
    sin_b = sine_table[:, None, :]
    return jnp.concatenate([first * cos_b - second * sin_b, second * cos_b + first * sin_b], axis=-1)

def attention_step(pieces):
    query_vectors, key_row_block, value_row_block, member = pieces
    count_of_rows = query_vectors.shape[0]
    group_factor = query_vectors.shape[1] // key_row_block.shape[1]
    key_full = jnp.repeat(key_row_block, group_factor, axis=1)
    value_full = jnp.repeat(value_row_block, group_factor, axis=1)
    scores = lower_precision_backward(jnp.einsum('qhd,khd->hqk', query_vectors, key_full, precision=highest) * query_vectors.shape[2] ** (-0.5))
    index_rows = jnp.arange(count_of_rows, dtype=jnp.int32)
    allowed = (member[:, None] == member[None, :]) & (index_rows[:, None] >= index_rows[None, :])
    scores = jnp.where(allowed[None], scores, -1e+30)
    probs = lower_precision(jax.nn.softmax(scores, axis=-1))
    return jnp.einsum('hqk,khd->qhd', probs, value_full, precision=highest)

def reference(tokens, lengths, routes, cotangent, gain_attn, w_query, key_projection_weight, value_projection_weight, w_out, gain_moe, w_router, w_gate, w_up, w_down):
    count_of_rows = TOK_DEV
    block_list = tokens.shape[0] // count_of_rows
    membership_total, position_all = jax.vmap(lambda row: positions_of(row, count_of_rows))(lengths)
    cosine_table, sine_table = rope_tables(position_all.reshape(-1), HEAD_DIMENSION)
    chosen = jax.nn.one_hot(routes, EXPERTS, dtype=jnp.float32)

    def forward(x_in, gain_one, query_w, key_weight_local, value_weight_local, out_w, gain_two, router_w, gate_w, up_w, down_w):
        count_total = x_in.shape[0]
        first_normalized = lower_precision(rms_scale(x_in, gain_one))
        query_before_rotation = lower_precision_backward(matrix_product(first_normalized, query_w)).reshape(count_total, QUERY_HEADS, HEAD_DIMENSION)
        key_before_rotation = lower_precision_backward(matrix_product(first_normalized, key_weight_local)).reshape(count_total, KEY_VALUE_HEADS, HEAD_DIMENSION)
        value_row_block = lower_precision(lower_precision_backward(matrix_product(first_normalized, value_weight_local))).reshape(count_total, KEY_VALUE_HEADS, HEAD_DIMENSION)
        query_vectors = lower_precision(apply_rotary(query_before_rotation, cosine_table, sine_table))
        key_row_block = lower_precision(apply_rotary(key_before_rotation, cosine_table, sine_table))
        head_list = lax.map(jax.checkpoint(attention_step), (query_vectors.reshape(block_list, count_of_rows, QUERY_HEADS, HEAD_DIMENSION), key_row_block.reshape(block_list, count_of_rows, KEY_VALUE_HEADS, HEAD_DIMENSION), value_row_block.reshape(block_list, count_of_rows, KEY_VALUE_HEADS, HEAD_DIMENSION), membership_total))
        attn_rows = lower_precision(lower_precision_backward(head_list.reshape(count_total, QUERY_HEADS * HEAD_DIMENSION)))
        resid = x_in + lower_precision_backward(matrix_product(attn_rows, out_w))
        normed_two = lower_precision(rms_scale(resid, gain_two))
        logits = lower_precision_backward(matrix_product(normed_two, router_w))
        picked = jnp.einsum('te,tke->tk', logits, chosen, precision=highest)
        gates = jax.nn.softmax(picked, axis=-1)
        share_all = jnp.einsum('tk,tke->et', gates, chosen, precision=highest)

        def one_expert(total, item):
            gate_mat, up_mat, down_mat, share = item
            copy_in = lower_precision_backward(normed_two)
            gate_pre = lower_precision_backward(matrix_product(copy_in, gate_mat))
            up_pre = lower_precision_backward(matrix_product(copy_in, up_mat))
            hidden = lower_precision(jax.nn.silu(gate_pre) * up_pre)
            result = lower_precision(lower_precision_backward(matrix_product(hidden, down_mat)))
            return (total + share[:, None] * result, None)
        moe, _ = lax.scan(jax.checkpoint(one_expert), jnp.zeros_like(x_in), (gate_w, up_w, down_w, share_all))
        return resid + moe
    inputs = tuple((item.astype(jnp.float32) for item in (tokens, gain_attn, w_query, key_projection_weight, value_projection_weight, w_out, gain_moe, w_router, w_gate, w_up, w_down)))
    result, pull = jax.vjp(forward, *inputs)
    grads = pull(cotangent.astype(jnp.float32))
    return (result.astype(jnp.bfloat16), grads[0].astype(jnp.bfloat16), grads[1], grads[2], grads[3], grads[4], grads[5], grads[6], grads[7], grads[8], grads[9], grads[10])
```

```python
import math

import jax
import jax.numpy as jnp
from jax import lax
from jax.experimental import pallas as pl
from jax.experimental.pallas import tpu as pltpu
from jax.sharding import PartitionSpec as P

QUERY_HEADS = 16
KEY_VALUE_HEADS = 8
HEAD_DIMENSION = 64


eps_norm = 1e-06


def positions_of(lengths_row, count_of_rows):
    index_rows = jnp.arange(count_of_rows, dtype=jnp.int32)
    ends = jnp.cumsum(lengths_row)
    member = jnp.sum((index_rows[:, None] >= ends[None, :]).astype(jnp.int32), axis=1)
    starts = ends - lengths_row
    onehot = member[:, None] == jnp.arange(lengths_row.shape[0], dtype=jnp.int32)[None, :]
    begin = jnp.sum(jnp.where(onehot, starts[None, :], 0), axis=1)
    return (member, index_rows - begin)


def rope_tables(positions, head_size):
    half_size = head_size // 2
    freq = jnp.exp(
        jnp.arange(half_size, dtype=jnp.float32) * (-2.0 * math.log(10000.0) / head_size)
    )
    angle = positions.astype(jnp.float32)[:, None] * freq[None, :]
    return (jnp.cos(angle), jnp.sin(angle))


def apply_rotary(values, cosine_table, sine_table):
    half_size = values.shape[-1] // 2
    first = values[..., :half_size]
    second = values[..., half_size:]
    cos_b = cosine_table[:, None, :]
    sin_b = sine_table[:, None, :]
    return jnp.concatenate(
        [first * cos_b - second * sin_b, second * cos_b + first * sin_b], axis=-1
    )


def reverse_rotary(grads, cosine_table, sine_table):
    half_size = grads.shape[-1] // 2
    first = grads[..., :half_size]
    second = grads[..., half_size:]
    cos_b = cosine_table[:, None, :]
    sin_b = sine_table[:, None, :]
    return jnp.concatenate(
        [first * cos_b + second * sin_b, second * cos_b - first * sin_b], axis=-1
    )


F32 = jnp.float32
BF16 = jnp.bfloat16
VMEM_LIMIT = 56 * 1024 * 1024


def hop(values, axis, mask):
    count = lax.axis_size(axis)
    return lax.ppermute(values, axis, [(i, i ^ mask) for i in range(count)])


def link_bits(count):
    return [1 << i for i in range(1, count.bit_length() - 1)]


def after(values, *earlier):
    return lax.optimization_barrier((values, *earlier))[0]


def spread_half(piece, count, order):
    blocks = {0: piece}
    for bit in order:
        for m in list(blocks):
            blocks[m ^ bit] = hop(blocks[m], "expert", bit)
    for m in list(blocks):
        blocks[m ^ 1] = hop(blocks[m], "expert", 1)
    return blocks


def gather_plane(first, second):
    count = lax.axis_size("expert")
    bits = link_bits(count)
    return spread_half(first, count, bits), spread_half(second, count, bits[::-1])


def gather_small(values):
    count = lax.axis_size("expert")
    rows = values[None]
    bit = 1
    while bit < count:
        rows = jnp.concatenate([rows, hop(rows, "expert", bit)], axis=0)
        bit *= 2
    return rows


def place_kernel(devices, count, rows, *refs):
    pieces, own_ref, out_ref, sems = refs[:-3], refs[-3], refs[-2], refs[-1]
    z_index = lax.axis_index("dp")
    e_index = lax.axis_index("expert")
    shard_rows = own_ref.shape[0]
    width = out_ref.shape[1]
    half = width // 2
    copies = [
        pltpu.make_async_copy(
            own_ref,
            out_ref.at[pl.ds(pl.multiple_of(z_index * shard_rows, 16), shard_rows), :],
            sems.at[0],
        )
    ]
    for side in range(2):
        for m in range(count):
            piece = pieces[side * count + m]
            for zm in range(1, devices):
                start = (z_index ^ zm) * shard_rows + (e_index ^ m) * rows
                copies.append(
                    pltpu.make_async_copy(
                        piece.at[pl.ds((zm - 1) * rows, rows), :],
                        out_ref.at[
                            pl.ds(pl.multiple_of(start, 16), rows), pl.ds(side * half, half)
                        ],
                        sems.at[len(copies)],
                    )
                )
    for copy in copies:
        copy.start()
    for copy in copies:
        copy.wait()


def gather_weight(shard):
    devices = lax.axis_size("dp")
    count = lax.axis_size("expert")
    shard_rows, width = shard.shape
    rows = shard_rows // count
    if rows % 16 or width % 256:
        return lax.all_gather(shard, "dp", axis=0, tiled=True)
    mine = lax.dynamic_slice_in_dim(shard, lax.axis_index("expert") * rows, rows, 0)
    far = jnp.concatenate([hop(mine, "dp", m) for m in range(1, devices)], axis=0)
    one, two = gather_plane(far[:, : width // 2], far[:, width // 2 :])
    pieces = [one[m] for m in range(count)] + [two[m] for m in range(count)]
    any_space = pl.BlockSpec(memory_space=pl.ANY)
    return pl.pallas_call(
        lambda *refs: place_kernel(devices, count, rows, *refs),
        out_shape=jax.ShapeDtypeStruct((shard_rows * devices, width), shard.dtype),
        in_specs=[any_space] * (len(pieces) + 1),
        out_specs=any_space,
        scratch_shapes=[pltpu.SemaphoreType.DMA((1 + 2 * count * (devices - 1),))],
        name="place_weight",
    )(*pieces, shard)


def bit_of(index, bit):
    return (index // bit) % 2


def reduce_weight(total):
    devices = lax.axis_size("dp")
    count = lax.axis_size("expert")
    height, width = total.shape
    rows = height // (devices * count)
    if rows % 16:
        part = lax.psum_scatter(total, "dp", scatter_dimension=0, tiled=True)
        return lax.psum(part, "expert").astype(F32)
    z_index = lax.axis_index("dp")
    e_index = lax.axis_index("expert")
    bits = [1 << i for i in range(count.bit_length() - 1)]
    levels = len(bits)

    def axis_of(bit):
        return levels - bit.bit_length() + 1

    def split(part, bit):
        mine = bit_of(e_index, bit)
        axis = axis_of(bit)
        send = lax.dynamic_index_in_dim(part, 1 - mine, axis, keepdims=True)
        keep = lax.dynamic_index_in_dim(part, mine, axis, keepdims=True)
        return (keep.astype(F32) + hop(send, "expert", bit).astype(F32)).astype(BF16)

    whole = total.reshape((devices,) + (2,) * levels + (rows, width))
    near = split(whole, 1)
    halves = [near[: devices // 2], near[devices // 2 :]]
    for side, order in enumerate((bits[1:], bits[1:][::-1])):
        for bit in order:
            halves[side] = split(halves[side], bit)
    line = jnp.concatenate(halves, axis=0).reshape(devices, rows, width)
    done = lax.dynamic_index_in_dim(line, z_index, 0, keepdims=False).astype(F32)
    for m in range(1, devices):
        piece = lax.dynamic_index_in_dim(line, z_index ^ m, 0, keepdims=False)
        done = done + hop(piece, "dp", m).astype(F32)
    done = done.astype(BF16)

    def join(part, bit):
        other = hop(part, "expert", bit)
        axis = axis_of(bit) - 1
        return jnp.where(
            bit_of(e_index, bit) == 0,
            jnp.concatenate([part, other], axis=axis),
            jnp.concatenate([other, part], axis=axis),
        )

    done = join(done.reshape((1,) * levels + (rows, width)), 1)
    sides = [done[..., : width // 2], done[..., width // 2 :]]
    for side, order in enumerate((bits[1:], bits[1:][::-1])):
        for bit in order:
            sides[side] = join(sides[side], bit)
    return jnp.concatenate(sides, axis=-1).reshape(count * rows, width).astype(F32)


def reduce_small(values):
    for axis in ("expert", "dp"):
        bit = 1
        while bit < lax.axis_size(axis):
            values = values + hop(values, axis, bit)
            bit *= 2
    return values


def scatter_line(pieces):
    devices = lax.axis_size("dp")
    z_index = lax.axis_index("dp")

    def at(index):
        return lax.dynamic_index_in_dim(pieces, index % devices, 0, keepdims=False)

    right = left = None
    for step in range(1, devices):
        give_right = at(z_index + devices - step)
        give_left = at(z_index + step)
        if right is not None:
            give_right = (give_right.astype(F32) + right.astype(F32)).astype(BF16)
            give_left = (give_left.astype(F32) + left.astype(F32)).astype(BF16)
        right = lax.ppermute(give_right, "dp", [(i, i + 1) for i in range(step) if i + 1 < devices])
        left = lax.ppermute(
            give_left, "dp", [(devices - 1 - i, devices - 2 - i) for i in range(step)]
        )
    return at(z_index).astype(F32) + right.astype(F32) + left.astype(F32)


def pick_rows(slots, capacity):
    index = lax.broadcasted_iota(jnp.int32, (capacity, slots.shape[1]), 0)
    return index == slots


def expert_kernel(capacity, *refs):
    tok, cot = refs[0:4], refs[4:8]
    slot_ref, route_ref, mine_ref, router_ref, gate_up_ref, down_ref = refs[8:14]
    (keep_moe, give_moe, keep_in, give_in, rows_ref, ge_ref, hid_ref, dgu_ref, gg_ref) = refs[14:23]
    drows_ref, chosen_ref, gg_col = refs[23:]
    half = tok[0].shape[0]
    lanes = mine_ref.shape[1]
    top = route_ref.shape[1]
    hidden_width = hid_ref.shape[1]
    for b in range(2):
        sel = pick_rows(slot_ref[b : b + 1, :], capacity).astype(F32).astype(BF16)
        place = pl.ds(b * capacity, capacity)
        for source, target in ((tok, rows_ref), (cot, drows_ref)):
            target[place, :] = (
                jnp.dot(sel[:, :half], source[2 * b][...], preferred_element_type=F32)
                + jnp.dot(sel[:, half:], source[2 * b + 1][...], preferred_element_type=F32)
            ).astype(BF16)
        expert = lax.broadcasted_iota(jnp.int32, (lanes, 2 * half), 0)
        named = route_ref[b, 0:1, :] == expert
        for k in range(1, top):
            named = named | (route_ref[b, k : k + 1, :] == expert)
        chosen_ref[place, :] = lax.dot_general(
            sel,
            named.astype(F32).astype(BF16),
            (((1,), (1,)), ((), ())),
            preferred_element_type=F32,
        )

    for b in range(2):
        place = pl.ds(b * capacity, capacity)
        rows = rows_ref[place, :]
        drows = drows_ref[place, :].astype(F32)
        logits = jnp.dot(rows, router_ref[...], preferred_element_type=F32)
        chosen = chosen_ref[place, :] > 0.5
        shown = jnp.where(chosen, logits, -1e30)
        weight = jnp.where(chosen, jnp.exp(shown - jnp.max(shown, axis=-1, keepdims=True)), 0.0)
        total = jnp.sum(weight, axis=-1, keepdims=True)
        gate = jnp.sum(weight * mine_ref[...], axis=-1, keepdims=True) / jnp.where(
            total > 0.0, total, 1.0
        )
        gate_up = jnp.dot(rows, gate_up_ref[...], preferred_element_type=F32)
        gate_pre = gate_up[:, :hidden_width]
        up_pre = gate_up[:, hidden_width:]
        sigm = 1.0 / (1.0 + jnp.exp(-gate_pre))
        activated = gate_pre * sigm
        hidden = (activated * up_pre).astype(BF16)
        hid_ref[place, :] = hidden
        result = jnp.dot(hidden, down_ref[...], preferred_element_type=F32)
        result = result.astype(BF16).astype(F32)
        gg_col[place, :] = jnp.sum(drows * result, axis=-1, keepdims=True)
        moe = (give_moe if b else keep_moe)
        moe[...] = (gate * result).astype(BF16)
        grad_out = (gate * drows).astype(BF16)
        ge_ref[place, :] = grad_out
        grad_hidden = lax.dot_general(
            grad_out, down_ref[...], (((1,), (1,)), ((), ())), preferred_element_type=F32
        )
        dgate = (grad_hidden * up_pre * sigm * (1.0 + gate_pre * (1.0 - sigm))).astype(BF16)
        dup = (grad_hidden * activated).astype(BF16)
        dgu_ref[place, :hidden_width] = dgate
        dgu_ref[place, hidden_width:] = dup
        grad_in = lax.dot_general(
            dgu_ref[place, :], gate_up_ref[...], (((1,), (1,)), ((), ())), preferred_element_type=F32
        )
        back = (give_in if b else keep_in)
        back[...] = grad_in.astype(BF16)
        picked = pick_rows(slot_ref[b : b + 1, :], capacity)
        gg_ref[b : b + 1, :] = jnp.sum(
            jnp.where(picked, gg_col[place, :], 0.0), axis=0, keepdims=True
        )


def expert_group(tok, cot, slots, routes, mine, router, gate_up, down, capacity):
    width = tok[0].shape[1]
    hidden = down.shape[0]
    tokens = slots.shape[1]
    low = lambda *shape: jax.ShapeDtypeStruct(shape, BF16)
    rows = 2 * capacity
    vmem = pl.BlockSpec(memory_space=pltpu.VMEM)
    flops = 2 * rows * width * hidden * 6 + 4 * rows * tokens * width
    return pl.pallas_call(
        lambda *refs: expert_kernel(capacity, *refs),
        out_shape=(
            low(capacity, width),
            low(capacity, width),
            low(capacity, width),
            low(capacity, width),
            low(rows, width),
            low(rows, width),
            low(rows, hidden),
            low(rows, 2 * hidden),
            jax.ShapeDtypeStruct((2, tokens), F32),
        ),
        in_specs=[vmem] * 14,
        out_specs=[vmem] * 9,
        scratch_shapes=[
            pltpu.VMEM((rows, width), BF16),
            pltpu.VMEM((rows, mine.shape[1]), F32),
            pltpu.VMEM((rows, 1), F32),
        ],
        compiler_params=pltpu.CompilerParams(vmem_limit_bytes=VMEM_LIMIT),
        cost_estimate=pl.CostEstimate(
            flops=flops, bytes_accessed=16 * 1024 * 1024, transcendentals=rows * hidden
        ),
        name="expert_group",
    )(*tok, *cot, slots, routes, mine, router, gate_up, down)


def combine_kernel(capacity, keep_ref, sib_ref, slot_ref, *outs):
    half = outs[0].shape[0]
    for side, out in enumerate(outs):
        total = None
        for who, rows in enumerate((keep_ref, sib_ref)):
            sel = pick_rows(slot_ref[who : who + 1, side * half : (side + 1) * half], capacity)
            part = lax.dot_general(
                sel.astype(F32).astype(BF16),
                rows[...],
                (((0,), (0,)), ((), ())),
                preferred_element_type=F32,
            )
            total = part if total is None else total + part
        out[...] = total.astype(BF16)


def combine(keep, sib, slots):
    capacity, width = keep.shape
    tokens = slots.shape[1]
    vmem = pl.BlockSpec(memory_space=pltpu.VMEM)
    return pl.pallas_call(
        lambda *refs: combine_kernel(capacity, *refs),
        out_shape=(jax.ShapeDtypeStruct((tokens // 2, width), BF16),) * 2,
        in_specs=[vmem] * 3,
        out_specs=[vmem] * 2,
        compiler_params=pltpu.CompilerParams(vmem_limit_bytes=VMEM_LIMIT),
        cost_estimate=pl.CostEstimate(
            flops=4 * tokens * capacity * width, bytes_accessed=2 * 1024 * 1024, transcendentals=0
        ),
        name="combine_rows",
    )(keep, sib, slots)


def wgrad_kernel(groups, gate_rows, down_rows, *refs):
    rows, ge, hid, dgu = (refs[i * groups : (i + 1) * groups] for i in range(4))
    out = refs[4 * groups]
    for left, right, start, count in (
        (rows, dgu, 0, gate_rows),
        (hid, ge, gate_rows, down_rows),
    ):
        total = None
        for g in range(groups):
            part = lax.dot_general(
                left[g][...], right[g][...], (((0,), (0,)), ((), ())), preferred_element_type=F32
            )
            total = part if total is None else total + part
        out[0, start : start + count, :] = total.astype(BF16)


def expert_wgrad(rows, ge, hid, dgu):
    devices = lax.axis_size("dp")
    groups = len(rows)
    width = rows[0].shape[1]
    hidden = hid[0].shape[1]
    gate_rows, down_rows = width // devices, hidden // devices
    if groups > 4 or gate_rows % 128 or down_rows % 128:
        everything = [jnp.concatenate(part, axis=0) for part in (rows, ge, hid, dgu)]
        gate_up = jnp.dot(everything[0].T, everything[3], preferred_element_type=F32)
        down = jnp.dot(everything[2].T, everything[1], preferred_element_type=F32)
        return jnp.concatenate(
            [
                gate_up.astype(BF16).reshape(devices, gate_rows, 2 * hidden),
                down.astype(BF16).reshape(devices, down_rows, width),
            ],
            axis=1,
        )
    count = rows[0].shape[0]
    sliced = lambda size: pl.BlockSpec((count, size), lambda i: (0, i))
    fixed = lambda size: pl.BlockSpec((count, size), lambda i: (0, 0))
    return pl.pallas_call(
        lambda *refs: wgrad_kernel(groups, gate_rows, down_rows, *refs),
        grid=(devices,),
        out_shape=jax.ShapeDtypeStruct((devices, gate_rows + down_rows, width), BF16),
        in_specs=[sliced(gate_rows)] * groups
        + [fixed(width)] * groups
        + [sliced(down_rows)] * groups
        + [fixed(2 * hidden)] * groups,
        out_specs=pl.BlockSpec((1, gate_rows + down_rows, width), lambda i: (i, 0, 0)),
        compiler_params=pltpu.CompilerParams(vmem_limit_bytes=VMEM_LIMIT),
        cost_estimate=pl.CostEstimate(
            flops=2 * groups * count * width * hidden * 3,
            bytes_accessed=16 * 1024 * 1024,
            transcendentals=0,
        ),
        name="expert_wgrad",
    )(*rows, *ge, *hid, *dgu)


def return_plane(partial):
    count = lax.axis_size("expert")
    bits = link_bits(count)
    results = []
    for side, order in enumerate((bits, bits[::-1])):
        blocks = {m: partial[m][side] for m in partial}
        for bit in order:
            arrived = {
                m: hop(blocks[m], "expert", bit) for m in sorted(blocks, reverse=True) if m & bit
            }
            blocks = {m: blocks[m] for m in blocks if not m & bit}
            if bit == order[-1]:
                results.append((blocks[0], arrived[bit]))
            else:
                blocks = {
                    m: (blocks[m].astype(F32) + arrived[m | bit].astype(F32)).astype(BF16)
                    for m in blocks
                }
    return results


def join_halves(results):
    return jnp.concatenate([a.astype(F32) + b.astype(F32) for a, b in results], axis=0)


def local(
    tokens,
    lengths,
    routes,
    cotangent,
    gain_attn,
    w_query,
    key_projection_weight,
    value_projection_weight,
    w_out,
    gain_moe,
    w_router,
    w_gate,
    w_up,
    w_down,
):
    single_float = F32
    brain_float_half = BF16
    count_of_rows, model_width = tokens.shape
    half_rows = count_of_rows // 2
    expert_count = lax.axis_size("expert")
    devices = lax.axis_size("dp")
    e_index = lax.axis_index("expert")
    z_index = lax.axis_index("dp")
    top_count = routes.shape[1]
    capacity = 2 * count_of_rows * top_count // expert_count
    group_factor = QUERY_HEADS // KEY_VALUE_HEADS
    scale = HEAD_DIMENSION ** (-0.5)
    shard_rows = gain_attn.shape[0]

    small = jnp.concatenate([gain_attn[None], gain_moe[None], w_router.T], axis=0)
    pad = -small.shape[0] % 16
    small = jnp.pad(small, ((0, pad), (0, 0)))
    small_all = jnp.stack([small] + [hop(small, "dp", m) for m in range(1, devices)])
    small_all = jnp.take(small_all, z_index ^ jnp.arange(devices), axis=0)
    small_all = small_all.transpose(1, 0, 2).reshape(small.shape[0], model_width)
    gain_first = small_all[0].astype(F32)
    gain_second = small_all[1].astype(F32)
    router_w = small_all[2 : 2 + expert_count].T
    lanes = -(-expert_count // 128) * 128
    router_wide = jnp.pad(router_w, ((0, 0), (0, lanes - expert_count)))

    qkv_w = gather_weight(
        jnp.concatenate([w_query, key_projection_weight, value_projection_weight], axis=1)
    )
    out_w = gather_weight(w_out)
    query_width = w_query.shape[1]
    key_width = key_projection_weight.shape[1]

    routes_rel = gather_small(routes.T)
    before = (
        jnp.arange(count_of_rows)[:, None] < jnp.arange(count_of_rows)[None, :]
    ).astype(BF16)

    def slots_of(expert):
        hit = jnp.any(routes_rel == expert, axis=1)
        place = jnp.dot(hit.astype(BF16), before, preferred_element_type=F32)
        return jnp.where(hit, place.astype(jnp.int32), -1)

    slots_mine = slots_of(e_index)
    slots_sibling = slots_of(e_index ^ 1)
    mine_row = (jnp.arange(lanes) == e_index).astype(F32)[None]
    gate_up_w = jnp.concatenate([w_gate[0], w_up[0]], axis=1)
    down_w = w_down[0]

    resid_in = tokens.astype(single_float)
    inverse_one = lax.rsqrt(jnp.mean(resid_in * resid_in, axis=-1, keepdims=True) + eps_norm)
    first_normalized = (resid_in * inverse_one * gain_first).astype(brain_float_half)
    qkv = jnp.dot(first_normalized, qkv_w, preferred_element_type=single_float)
    query_before_rotation = qkv[:, :query_width].reshape(
        count_of_rows, QUERY_HEADS, HEAD_DIMENSION
    )
    key_before_rotation = qkv[:, query_width : query_width + key_width].reshape(
        count_of_rows, KEY_VALUE_HEADS, HEAD_DIMENSION
    )
    value_before_mixing = qkv[:, query_width + key_width :]
    cot_one, cot_two = gather_plane(
        after(cotangent[:half_rows], qkv_w), after(cotangent[half_rows:], qkv_w)
    )
    member, position = positions_of(lengths[0], count_of_rows)
    cosine_table, sine_table = rope_tables(position, HEAD_DIMENSION)
    query_vectors = (
        apply_rotary(query_before_rotation, cosine_table, sine_table)
        .astype(brain_float_half)
        .reshape(count_of_rows, KEY_VALUE_HEADS, group_factor, HEAD_DIMENSION)
    )
    key_row_block = apply_rotary(key_before_rotation, cosine_table, sine_table).astype(
        brain_float_half
    )
    value_row_block = value_before_mixing.astype(brain_float_half).reshape(
        count_of_rows, KEY_VALUE_HEADS, HEAD_DIMENSION
    )
    index_rows = jnp.arange(count_of_rows, dtype=jnp.int32)
    allowed = (member[:, None] == member[None, :]) & (index_rows[:, None] >= index_rows[None, :])

    def masked_scores():
        raw_scores = (
            jnp.einsum(
                "qcgd,kcd->cgqk", query_vectors, key_row_block, preferred_element_type=single_float
            )
            * scale
        )
        return jnp.where(allowed, raw_scores, -1e30)

    scores = masked_scores()
    row_peak = jnp.max(scores, axis=-1, keepdims=True)
    shifted_exp = jnp.exp(scores - row_peak)
    row_total = jnp.sum(shifted_exp, axis=-1, keepdims=True)
    probs = (shifted_exp / row_total).astype(brain_float_half)
    log_total = row_peak + jnp.log(row_total)
    mixed_heads = jnp.einsum(
        "cgqk,kcd->qcgd", probs, value_row_block, preferred_element_type=single_float
    )
    attn_rows = mixed_heads.reshape(count_of_rows, QUERY_HEADS * HEAD_DIMENSION).astype(
        brain_float_half
    )
    resid_mid = resid_in + jnp.dot(attn_rows, out_w, preferred_element_type=single_float)
    inverse_two = lax.rsqrt(jnp.mean(resid_mid * resid_mid, axis=-1, keepdims=True) + eps_norm)
    normed_two = (resid_mid * inverse_two * gain_second).astype(brain_float_half)

    tok_one, tok_two = gather_plane(normed_two[:half_rows], normed_two[half_rows:])

    logits = jnp.dot(normed_two, router_w, preferred_element_type=single_float)
    expert_ids = jnp.arange(expert_count, dtype=jnp.int32)
    chosen = (routes[:, :, None] == expert_ids[None, None, :]).astype(single_float)
    picked = jnp.sum(logits[:, None, :] * chosen, axis=-1)
    gates = jax.nn.softmax(picked, axis=-1)

    moe_partial, in_partial, saved, gg_rows = {}, {}, [], {}
    pending = {}
    for low_mask in range(0, expert_count, 2):
        pair = (low_mask, low_mask ^ 1)
        tok = [side[m] for m in pair for side in (tok_one, tok_two)]
        cot = [side[m] for m in pair for side in (cot_one, cot_two)]
        keep_moe, give_moe, keep_in, give_in, rows, ge, hid, dgu, gg = expert_group(
            tok,
            cot,
            slots_mine[low_mask : low_mask + 2],
            routes_rel[low_mask : low_mask + 2],
            mine_row,
            router_wide,
            gate_up_w,
            down_w,
            capacity,
        )
        saved.append((rows, ge, hid, dgu))
        slots = jnp.stack([slots_mine[low_mask], slots_sibling[low_mask]])
        in_partial[low_mask] = combine(keep_in, hop(give_in, "expert", 1), slots)
        pending[low_mask] = (keep_moe, give_moe, slots)
        gg_rows[low_mask] = gg[0]
        gg_rows[low_mask ^ 1] = gg[1]

    grad_result = return_plane(in_partial)
    gg_all = jnp.stack(
        [gg_rows[0]] + [hop(gg_rows[m], "expert", m) for m in range(1, expert_count)]
    )
    for low_mask, (keep_moe, give_moe, slots) in pending.items():
        give_moe = after(give_moe, *[r[1] for r in grad_result])
        moe_partial[low_mask] = combine(keep_moe, hop(give_moe, "expert", 1), slots)
    moe_result = return_plane(moe_partial)
    mixed_out = (resid_mid + join_halves(moe_result)).astype(brain_float_half)

    expert_pieces = scatter_line(expert_wgrad(*[list(part) for part in zip(*saved)]))

    grad_final = cotangent.astype(single_float)
    owner = (e_index ^ jnp.arange(expert_count))[:, None, None]
    grad_gates = jnp.sum(
        jnp.where(routes.T[None] == owner, gg_all[:, None, :], 0.0), axis=0
    ).T
    grad_picked = gates * (grad_gates - jnp.sum(gates * grad_gates, axis=-1, keepdims=True))
    grad_logits = jnp.sum(grad_picked[:, :, None] * chosen, axis=1).astype(brain_float_half)
    grad_router_w = lax.dot_general(
        grad_logits, normed_two, (((0,), (0,)), ((), ())), preferred_element_type=single_float
    )
    grad_normed_two = jnp.dot(grad_logits, router_w.T, preferred_element_type=single_float)
    grad_normed_two = grad_normed_two + join_halves(grad_result)
    scaled_two = grad_normed_two * gain_second
    grad_gain_two = jnp.sum(grad_normed_two * resid_mid * inverse_two, axis=0)
    grad_mid = (
        grad_final
        + inverse_two * scaled_two
        - resid_mid
        * inverse_two
        * inverse_two
        * inverse_two
        * jnp.mean(resid_mid * scaled_two, axis=-1, keepdims=True)
    )
    grad_mid_low = grad_mid.astype(brain_float_half)
    grad_out_w = jnp.dot(attn_rows.T, grad_mid_low, preferred_element_type=single_float)
    grad_attn = (
        lax.dot_general(
            grad_mid_low, out_w, (((1,), (1,)), ((), ())), preferred_element_type=single_float
        )
        .astype(brain_float_half)
        .reshape(count_of_rows, KEY_VALUE_HEADS, group_factor, HEAD_DIMENSION)
    )
    grad_out_part = reduce_weight(grad_out_w.astype(BF16))
    small_grads = reduce_small(jnp.concatenate([grad_gain_two[None], grad_router_w], axis=0))
    scores_again = masked_scores()
    probs_again = jnp.exp(scores_again - log_total)
    grad_probs = jnp.einsum(
        "qcgd,kcd->cgqk", grad_attn, value_row_block, preferred_element_type=single_float
    )
    delta_rows = jnp.sum(probs_again * grad_probs, axis=-1, keepdims=True)
    grad_scores = (probs_again * (grad_probs - delta_rows)).astype(brain_float_half)
    grad_query = (
        jnp.einsum(
            "cgqk,kcd->qcgd", grad_scores, key_row_block, preferred_element_type=single_float
        )
        * scale
    ).reshape(count_of_rows, QUERY_HEADS, HEAD_DIMENSION)
    key_matrix_gradient = (
        jnp.einsum(
            "cgqk,qcgd->kcd", grad_scores, query_vectors, preferred_element_type=single_float
        )
        * scale
    )
    value_matrix_gradient = jnp.einsum(
        "cgqk,qcgd->kcd",
        probs_again.astype(brain_float_half),
        grad_attn,
        preferred_element_type=single_float,
    )
    grad_query_pre = (
        reverse_rotary(grad_query, cosine_table, sine_table)
        .reshape(count_of_rows, QUERY_HEADS * HEAD_DIMENSION)
        .astype(brain_float_half)
    )
    key_before_gradient = (
        reverse_rotary(key_matrix_gradient, cosine_table, sine_table)
        .reshape(count_of_rows, KEY_VALUE_HEADS * HEAD_DIMENSION)
        .astype(brain_float_half)
    )
    value_before_gradient = value_matrix_gradient.reshape(
        count_of_rows, KEY_VALUE_HEADS * HEAD_DIMENSION
    ).astype(brain_float_half)
    grad_qkv = jnp.concatenate(
        [grad_query_pre, key_before_gradient, value_before_gradient], axis=1
    )
    grad_qkv_w = lax.dot_general(
        first_normalized, grad_qkv, (((0,), (0,)), ((), ())), preferred_element_type=single_float
    )
    qkv_part = reduce_weight(grad_qkv_w.astype(BF16))
    grad_normed_one = lax.dot_general(
        grad_qkv, qkv_w, (((1,), (1,)), ((), ())), preferred_element_type=single_float
    )
    scaled_one = grad_normed_one * gain_first
    grad_gain_one = jnp.sum(grad_normed_one * resid_in * inverse_one, axis=0)
    grad_input = (
        grad_mid
        + inverse_one * scaled_one
        - resid_in
        * inverse_one
        * inverse_one
        * inverse_one
        * jnp.mean(resid_in * scaled_one, axis=-1, keepdims=True)
    )
    gain_one_all = reduce_small(grad_gain_one[None])

    def own_part(values):
        return lax.dynamic_slice_in_dim(values, z_index * shard_rows, shard_rows, 1)

    small_part = own_part(small_grads)
    gate_rows = model_width // devices
    hidden = down_w.shape[0]
    return (
        mixed_out,
        grad_input.astype(brain_float_half),
        own_part(gain_one_all)[0],
        qkv_part[:, :query_width],
        qkv_part[:, query_width : query_width + key_width],
        qkv_part[:, query_width + key_width :],
        grad_out_part,
        small_part[0],
        small_part[1:].T,
        expert_pieces[None, :gate_rows, :hidden],
        expert_pieces[None, :gate_rows, hidden:],
        expert_pieces[None, gate_rows:, :],
    )


def solution(mesh):
    placed = (
        P(("dp", "expert"), None),
        P(("dp", "expert"), None),
        P(("dp", "expert"), None),
        P(("dp", "expert"), None),
        P("dp"),
        P("dp", None),
        P("dp", None),
        P("dp", None),
        P("dp", None),
        P("dp"),
        P("dp", None),
        P("expert", None, None),
        P("expert", None, None),
        P("expert", None, None),
    )
    return jax.shard_map(
        local,
        mesh=mesh,
        in_specs=placed,
        out_specs=(
            P(("dp", "expert"), None),
            P(("dp", "expert"), None),
            P("dp"),
            P("dp", None),
            P("dp", None),
            P("dp", None),
            P("dp", None),
            P("dp"),
            P("dp", None),
            P("expert", "dp", None),
            P("expert", "dp", None),
            P("expert", "dp", None),
        ),
        check_vma=False,
    )
```

```python
import math

import jax
import jax.numpy as jnp
from jax import lax
from jax.experimental import pallas as pl
from jax.experimental.pallas import tpu as pltpu
from jax.sharding import PartitionSpec as P

QUERY_HEADS = 16
KEY_VALUE_HEADS = 8
HEAD_DIMENSION = 64


eps_norm = 1e-06


def positions_of(lengths_row, count_of_rows):
    index_rows = jnp.arange(count_of_rows, dtype=jnp.int32)
    ends = jnp.cumsum(lengths_row)
    member = jnp.sum((index_rows[:, None] >= ends[None, :]).astype(jnp.int32), axis=1)
    starts = ends - lengths_row
    onehot = member[:, None] == jnp.arange(lengths_row.shape[0], dtype=jnp.int32)[None, :]
    begin = jnp.sum(jnp.where(onehot, starts[None, :], 0), axis=1)
    return (member, index_rows - begin)


def rope_tables(positions, head_size):
    half_size = head_size // 2
    freq = jnp.exp(
        jnp.arange(half_size, dtype=jnp.float32) * (-2.0 * math.log(10000.0) / head_size)
    )
    angle = positions.astype(jnp.float32)[:, None] * freq[None, :]
    return (jnp.cos(angle), jnp.sin(angle))


F32 = jnp.float32
BF16 = jnp.bfloat16
VMEM_LIMIT = 56 * 1024 * 1024
NT = (((1,), (1,)), ((), ()))
TN = (((0,), (0,)), ((), ()))


def lasting(microseconds):
    return pl.CostEstimate(
        flops=int(microseconds * 1.15e9), bytes_accessed=1 << 20, transcendentals=0
    )


def hop(values, axis, mask):
    count = lax.axis_size(axis)
    return lax.ppermute(values, axis, [(i, i ^ mask) for i in range(count)])


def after_all(values, *earlier):
    return list(lax.optimization_barrier((*values, *earlier))[: len(values)])


def link_bits(count):
    return [1 << i for i in range(1, count.bit_length() - 1)]


def after(values, *earlier):
    return lax.optimization_barrier((values, *earlier))[0]


def mixed_hop(values, first, second):
    count = lax.axis_size("expert")
    return lax.ppermute(
        values, "expert", [(i, i ^ (second if i % 2 else first)) for i in range(count)]
    )


def gather_links(block, hold=lambda pair: pair):
    count = lax.axis_size("expert")
    blocks = {0: block}
    if count == 8:
        blocks[2], blocks[4] = hold((hop(block, "expert", 2), hop(block, "expert", 4)))
        parity = lax.axis_index("expert") % 2
        blocks[6] = mixed_hop(jnp.where(parity == 0, blocks[2], blocks[4]), 4, 2)
        return blocks
    for bit in link_bits(count):
        for m in list(blocks):
            blocks[m ^ bit] = hop(blocks[m], "expert", bit)
    return blocks


def gather_plane(block):
    blocks = gather_links(block)
    for m in list(blocks):
        blocks[m ^ 1] = hop(blocks[m], "expert", 1)
    return blocks


def gather_small(values):
    count = lax.axis_size("expert")
    rows = values[None]
    bit = 1
    while bit < count:
        rows = jnp.concatenate([rows, hop(rows, "expert", bit)], axis=0)
        bit *= 2
    return rows


def place_kernel(devices, rows, *refs):
    near, own_ref, outs = refs[:-4], refs[-4], refs[-3:]
    z_index = lax.axis_index("dp")
    e_index = lax.axis_index("expert")
    shard_rows = own_ref.shape[0]

    def put(at, count, values):
        column = 0
        for out in outs:
            width = out.shape[1]
            out[pl.ds(pl.multiple_of(at, 16), count), :] = values[:, column : column + width]
            column += width

    put(z_index * shard_rows, shard_rows, own_ref[...])
    for m, block in enumerate(near):
        for zm in range(1, devices):
            at = (z_index ^ zm) * shard_rows + (e_index ^ m) * rows
            put(at, rows, block[(zm - 1) * rows : zm * rows, :])


def gather_weights(shards, widths, cotangent):
    devices = lax.axis_size("dp")
    count = lax.axis_size("expert")
    shard_rows = shards[0].shape[0]
    rows = shard_rows // count
    if rows % 16 or count != 8:
        whole = lax.all_gather(jnp.concatenate(shards, axis=1), "dp", axis=0, tiled=True)
        starts = [sum(widths[:i]) for i in range(len(widths))]
        arrays = [whole[:, s : s + w] for s, w in zip(starts, widths)]
        return arrays, gather_plane(cotangent), whole
    start = lax.axis_index("expert") * rows
    mine = jnp.concatenate(
        [lax.dynamic_slice_in_dim(shard, start, rows, 0) for shard in shards], axis=1
    )
    far = jnp.concatenate([hop(mine, "dp", m) for m in range(1, devices)], axis=0)
    cotangent = after(cotangent, mine)
    cot = {0: cotangent, 2: hop(cotangent, "expert", 2), 4: hop(cotangent, "expert", 4)}
    far = after(far, cot[2], cot[4])
    near = gather_links(far)
    for m in (0, 2, 4):
        near[m ^ 1] = hop(near[m], "expert", 1)
    near[7] = hop(after(near[6], near[1], near[3], near[5]), "expert", 1)
    parity = lax.axis_index("expert") % 2
    cot[6] = mixed_hop(after(jnp.where(parity == 0, cot[2], cot[4]), near[6]), 4, 2)
    for m in list(cot):
        cot[m ^ 1] = hop(after(cot[m], near[7]), "expert", 1)
    vmem = pl.BlockSpec(memory_space=pltpu.VMEM)
    arrays = pl.pallas_call(
        lambda *refs: place_kernel(devices, rows, *refs),
        out_shape=[
            jax.ShapeDtypeStruct((shard_rows * devices, width), mine.dtype) for width in widths
        ],
        in_specs=[vmem] * (count + 1),
        out_specs=[vmem] * len(widths),
        compiler_params=pltpu.CompilerParams(vmem_limit_bytes=VMEM_LIMIT),
        cost_estimate=lasting(6.0),
        name="place_weights",
    )(*[near[m] for m in range(count)], jnp.concatenate(shards, axis=1))
    return arrays, cot, near[7]


def split_kernel(columns, *refs):
    keep_ref, send_ref = refs[-2:]
    core = lax.axis_index("expert") % 2
    rows = keep_ref.shape[0] * 2
    group = rows // (lax.axis_size("dp") * lax.axis_size("expert"))
    start = at = 0
    for width, terms in columns:
        total = None
        for _ in range(terms):
            part = lax.dot_general(
                refs[at][...], refs[at + 1][...], TN, preferred_element_type=F32
            )
            total = part if total is None else total + part
            at += 2
        low = total.astype(BF16)
        place = slice(start, start + width)
        start += width
        for who, (even, odd) in enumerate(((keep_ref, send_ref), (send_ref, keep_ref))):

            @pl.when(core == who)
            def _(even=even, odd=odd, low=low, place=place):
                for i in range(rows // group):
                    out = odd if i % 2 else even
                    out[i // 2 * group : (i // 2 + 1) * group, place] = low[
                        i * group : (i + 1) * group, :
                    ]


def reduce_grads(columns):
    devices = lax.axis_size("dp")
    count = lax.axis_size("expert")
    height = columns[0][0][0].shape[1]
    rows = height // (devices * count)
    widths = [terms[0][1].shape[1] for terms in columns]
    width = sum(widths)
    if rows % 16:
        products = [
            sum(lax.dot_general(a, c, TN, preferred_element_type=F32) for a, c in terms)
            for terms in columns
        ]
        total = jnp.concatenate(products, axis=1).astype(BF16)

        return total, (lambda hold, *earlier: total, lambda whole, hold: whole)
    z_index = lax.axis_index("dp")
    e_index = lax.axis_index("expert")
    core, chip, chips = e_index % 2, e_index // 2, count // 2

    def pick(values, index, axis):
        return lax.dynamic_index_in_dim(values, index, axis, keepdims=False)

    vmem = pl.BlockSpec(memory_space=pltpu.VMEM)
    operands = [array for terms in columns for pair in terms for array in pair]
    depth = operands[0].shape[0]
    shape = tuple((w, len(terms)) for w, terms in zip(widths, columns))
    keep, send = pl.pallas_call(
        lambda *refs: split_kernel(shape, *refs),
        out_shape=(jax.ShapeDtypeStruct((height // 2, width), BF16),) * 2,
        in_specs=[vmem] * len(operands),
        out_specs=(vmem, vmem),
        compiler_params=pltpu.CompilerParams(vmem_limit_bytes=VMEM_LIMIT),
        cost_estimate=lasting(1.0 + 5.0 * width / height),
        name="weight_grads",
    )(*operands)

    def across_cores(hold, *earlier):
        arrived = hop(after(send, *earlier) if earlier else send, "expert", 1)
        near = hold(keep.astype(F32) + arrived.astype(F32)).astype(BF16)
        return near.reshape(devices, chips, rows, width)

    def across_links(near, hold):
        pieces = [
            hop(pick(near, chip ^ m, 1), "expert", 2 * m).astype(F32) for m in range(1, chips)
        ]
        line = pick(near, chip, 1).astype(F32)
        for piece in hold(pieces):
            line = line + piece
        return line.astype(BF16)

    return send, (across_cores, across_links)


def reduce_dp(line, height):
    devices = lax.axis_size("dp")
    count = lax.axis_size("expert")
    if line.ndim == 2:
        part = lax.psum_scatter(line, "dp", scatter_dimension=0, tiled=True)
        return lax.psum(part, "expert")
    z_index = lax.axis_index("dp")
    chip, chips = lax.axis_index("expert") // 2, count // 2
    rows, width = line.shape[1:]
    done = lax.dynamic_index_in_dim(line, z_index, 0, keepdims=False).astype(F32)
    for m in range(1, devices):
        piece = lax.dynamic_index_in_dim(line, z_index ^ m, 0, keepdims=False)
        done = done + hop(piece, "dp", m).astype(F32)
    done = done.astype(BF16)
    across = jnp.stack([done] + [hop(done, "expert", 2 * m) for m in range(1, chips)])
    across = jnp.take(across, chip ^ jnp.arange(chips), axis=0)
    other = hop(across, "expert", 1)
    both = jnp.where(
        lax.axis_index("expert") % 2 == 0,
        jnp.stack([across, other], axis=1),
        jnp.stack([other, across], axis=1),
    )
    return both.reshape(count * rows, width)


def pick_rows(slots, capacity):
    index = lax.broadcasted_iota(jnp.int32, (capacity, slots.shape[1]), 0)
    return index == slots


def expert_kernel(capacity, *refs):
    tok_hbm, cot_hbm = refs[0:2], refs[2:4]
    slot_ref, route_ref, mine_ref = refs[4:7]
    weights_hbm = refs[7:10]
    outs = refs[10:18]
    tok, cot, weights = refs[18:20], refs[20:22], refs[22:25]
    stores = refs[25:33]
    chosen_ref, sems = refs[33:]
    router_ref, gate_up_ref, down_ref = weights
    keep_moe, give_moe, keep_in, give_in, rows_ref, ge_ref, hid_ref, dgu_ref = stores
    pairs = [
        (tok_hbm[0], tok[0]),
        (cot_hbm[0], cot[0]),
        (weights_hbm[0], weights[0]),
        (weights_hbm[1], weights[1]),
        (tok_hbm[1], tok[1]),
        (cot_hbm[1], cot[1]),
        (weights_hbm[2], weights[2]),
    ]
    loads = [
        pltpu.make_async_copy(source, target, sems.at[i])
        for i, (source, target) in enumerate(pairs)
    ]
    for load in loads:
        load.start()
    writes = []

    def write(index, place=None):
        source, target = stores[index], outs[index]
        if place is not None:
            source, target = source.at[place, :], target.at[place, :]
        copy = pltpu.make_async_copy(source, target, sems.at[len(loads) + len(writes)])
        copy.start()
        writes.append(copy)

    tokens = tok[0].shape[0]
    lanes = mine_ref.shape[1]
    top = route_ref.shape[1]
    hidden_width = hid_ref.shape[1]
    for b in range(2):
        place = pl.ds(b * capacity, capacity)
        loads[4 * b].wait()
        picked = pick_rows(slot_ref[b : b + 1, :], capacity)
        sel = picked.astype(F32).astype(BF16)
        rows = jnp.dot(sel, tok[b][...], preferred_element_type=F32).astype(BF16)
        rows_ref[place, :] = rows
        write(4, place)
        loads[4 * b + 1].wait()
        drows = jnp.dot(sel, cot[b][...], preferred_element_type=F32)
        expert = lax.broadcasted_iota(jnp.int32, (lanes, tokens), 0)
        named = route_ref[b, 0:1, :] == expert
        for k in range(1, top):
            named = named | (route_ref[b, k : k + 1, :] == expert)
        chosen_ref[...] = lax.dot_general(
            sel, named.astype(F32).astype(BF16), NT, preferred_element_type=F32
        )
        if b == 0:
            loads[2].wait()
        logits = jnp.dot(rows, router_ref[...], preferred_element_type=F32)
        chosen = chosen_ref[...] > 0.5
        shown = jnp.where(chosen, logits, -1e30)
        weight = jnp.where(chosen, jnp.exp(shown - jnp.max(shown, axis=-1, keepdims=True)), 0.0)
        total = jnp.sum(weight, axis=-1, keepdims=True)
        gate = jnp.sum(weight * mine_ref[...], axis=-1, keepdims=True) / jnp.where(
            total > 0.0, total, 1.0
        )
        grad_out = (gate * drows).astype(BF16)
        ge_ref[place, :] = grad_out
        write(5, place)
        if b == 0:
            loads[3].wait()
        gate_up = jnp.dot(rows, gate_up_ref[...], preferred_element_type=F32)
        gate_pre = gate_up[:, :hidden_width]
        up_pre = gate_up[:, hidden_width:]
        if b == 0:
            loads[6].wait()
        grad_hidden = lax.dot_general(grad_out, down_ref[...], NT, preferred_element_type=F32)
        sigm = 1.0 / (1.0 + jnp.exp(-gate_pre))
        activated = gate_pre * sigm
        hidden = (activated * up_pre).astype(BF16)
        hid_ref[place, :] = hidden
        write(6, place)
        dgate = (grad_hidden * up_pre * sigm * (1.0 + gate_pre * (1.0 - sigm))).astype(BF16)
        dup = (grad_hidden * activated).astype(BF16)
        dgu_ref[place, :hidden_width] = dgate
        dgu_ref[place, hidden_width:] = dup
        write(7, place)
        back = give_in if b else keep_in
        width = rows.shape[1]
        back[:, :width] = lax.dot_general(
            dgu_ref[place, :], gate_up_ref[...], NT, preferred_element_type=F32
        ).astype(BF16)
        result = jnp.dot(hidden, down_ref[...], preferred_element_type=F32)
        result = result.astype(BF16).astype(F32)
        moe = give_moe if b else keep_moe
        moe[...] = (gate * result).astype(BF16)
        write(b)
        gate_grad = jnp.sum(drows * result, axis=-1, keepdims=True)
        high = gate_grad.astype(BF16).astype(F32)
        mine = mine_ref[...]
        back[:, width:] = (
            high * mine + (gate_grad - high) * pltpu.roll(mine, lanes // 2, 1)
        ).astype(BF16)
        write(2 + b)
    for copy in writes:
        copy.wait()


def expert_group(tok, cot, slots, routes, mine, router, gate_up, down, capacity):
    width = tok[0].shape[1]
    hidden = down.shape[0]
    tokens = slots.shape[1]
    rows = 2 * capacity
    vmem = pl.BlockSpec(memory_space=pltpu.VMEM)
    far = pl.BlockSpec(memory_space=pl.ANY)
    wide = width + mine.shape[1]
    shapes = [(capacity, width)] * 2 + [(capacity, wide)] * 2
    shapes += [(rows, width), (rows, width), (rows, hidden)]
    shapes.append((rows, 2 * hidden))
    return pl.pallas_call(
        lambda *refs: expert_kernel(capacity, *refs),
        out_shape=[jax.ShapeDtypeStruct(shape, BF16) for shape in shapes],
        in_specs=[far] * 4 + [vmem] * 3 + [far] * 3,
        out_specs=[far] * 8,
        scratch_shapes=[pltpu.VMEM((tokens, width), BF16)] * 4
        + [pltpu.VMEM(array.shape, BF16) for array in (router, gate_up, down)]
        + [pltpu.VMEM(shape, BF16) for shape in shapes]
        + [
            pltpu.VMEM((capacity, mine.shape[1]), F32),
            pltpu.SemaphoreType.DMA((7 + 12,)),
        ],
        compiler_params=pltpu.CompilerParams(vmem_limit_bytes=VMEM_LIMIT),
        cost_estimate=lasting(10.5),
        name="expert_group",
    )(*tok, *cot, slots, routes, mine, router, gate_up, down)


def combine_kernel(capacity, blocks, *refs):
    slot_refs = refs[2 * blocks : 3 * blocks]
    outs = refs[3 * blocks :]
    for i in range(blocks):
        total = None
        for who, rows in enumerate(refs[2 * i : 2 * i + 2]):
            sel = pick_rows(slot_refs[i][who : who + 1, :], capacity).astype(F32).astype(BF16)
            part = lax.dot_general(sel, rows[...], TN, preferred_element_type=F32)
            total = part if total is None else total + part
        outs[i][...] = total.astype(BF16)


def combine(rows, slots):
    blocks = len(slots)
    capacity, width = rows[0].shape
    tokens = slots[0].shape[1]
    vmem = pl.BlockSpec(memory_space=pltpu.VMEM)
    return pl.pallas_call(
        lambda *refs: combine_kernel(capacity, blocks, *refs),
        out_shape=[jax.ShapeDtypeStruct((tokens, width), BF16)] * blocks,
        in_specs=[vmem] * (3 * blocks),
        out_specs=[vmem] * blocks,
        compiler_params=pltpu.CompilerParams(vmem_limit_bytes=VMEM_LIMIT),
        cost_estimate=lasting(1.5 + 1.1 * blocks),
        name="combine_rows",
    )(*rows, *slots)


def wgrad_kernel(groups, gate_rows, down_rows, *refs):
    rows, ge, hid, dgu = (refs[i * groups : (i + 1) * groups] for i in range(4))
    out = refs[4 * groups]
    for left, right, start, count in (
        (rows, dgu, 0, gate_rows),
        (hid, ge, gate_rows, down_rows),
    ):
        total = None
        for g in range(groups):
            part = lax.dot_general(
                left[g][...], right[g][...], (((0,), (0,)), ((), ())), preferred_element_type=F32
            )
            total = part if total is None else total + part
        out[0, start : start + count, :] = total.astype(BF16)


def expert_wgrad(rows, ge, hid, dgu):
    devices = lax.axis_size("dp")
    groups = len(rows)
    width = rows[0].shape[1]
    hidden = hid[0].shape[1]
    gate_rows, down_rows = width // devices, hidden // devices
    if groups > 4 or gate_rows % 128 or down_rows % 128:
        everything = [jnp.concatenate(part, axis=0) for part in (rows, ge, hid, dgu)]
        gate_up = jnp.dot(everything[0].T, everything[3], preferred_element_type=F32)
        down = jnp.dot(everything[2].T, everything[1], preferred_element_type=F32)
        return jnp.concatenate(
            [
                gate_up.astype(BF16).reshape(devices, gate_rows, 2 * hidden),
                down.astype(BF16).reshape(devices, down_rows, width),
            ],
            axis=1,
        )
    count = rows[0].shape[0]
    sliced = lambda size: pl.BlockSpec((count, size), lambda i: (0, i))
    fixed = lambda size: pl.BlockSpec((count, size), lambda i: (0, 0))
    return pl.pallas_call(
        lambda *refs: wgrad_kernel(groups, gate_rows, down_rows, *refs),
        grid=(devices,),
        out_shape=jax.ShapeDtypeStruct((devices, gate_rows + down_rows, width), BF16),
        in_specs=[sliced(gate_rows)] * groups
        + [fixed(width)] * groups
        + [sliced(down_rows)] * groups
        + [fixed(2 * hidden)] * groups,
        out_specs=pl.BlockSpec((1, gate_rows + down_rows, width), lambda i: (i, 0, 0)),
        compiler_params=pltpu.CompilerParams(vmem_limit_bytes=VMEM_LIMIT),
        cost_estimate=lasting(12.5),
        name="expert_wgrad",
    )(*rows, *ge, *hid, *dgu)


def return_direct(partial):
    parity = lax.axis_index("expert") % 2
    return jnp.where(parity == 0, partial[2], partial[4])


def return_passed(partial):
    return mixed_hop(partial[6], 2, 4)


def return_onward(partial, passed):
    parity = lax.axis_index("expert") % 2
    rest = jnp.where(parity == 0, partial[4], partial[2]).astype(F32) + passed.astype(F32)
    return rest.astype(BF16)


def return_halving(partial):
    blocks = dict(partial)
    for bit in link_bits(lax.axis_size("expert")):
        arrived = {m: hop(blocks[m], "expert", bit) for m in blocks if m & bit}
        blocks = {
            m: (blocks[m].astype(F32) + arrived[m | bit].astype(F32)).astype(BF16)
            for m in blocks
            if not m & bit
        }
    return [blocks[0]]


def sum_terms(terms):
    total = terms[0].astype(F32)
    for term in terms[1:]:
        total = total + term.astype(F32)
    return total


def swap_halves(values):
    width = values.shape[1]
    half = HEAD_DIMENSION // 2
    lane = lax.broadcasted_iota(jnp.int32, values.shape, 1) % HEAD_DIMENSION
    return jnp.where(
        lane < half, pltpu.roll(values, width - half, 1), pltpu.roll(values, half, 1)
    )


def project_kernel(key_width, x_ref, gain_ref, w_ref, cos_ref, sin_ref, out_ref, xn_ref):
    step = pl.program_id(0)
    width = out_ref.shape[1]

    @pl.when(step == 0)
    def _():
        x = x_ref[...].astype(F32)
        inverse = lax.rsqrt(jnp.mean(x * x, axis=-1, keepdims=True) + eps_norm)
        xn_ref[...] = (x * inverse * gain_ref[...]).astype(BF16)

    before = jnp.dot(xn_ref[...], w_ref[...], preferred_element_type=F32)

    def turn(values):
        repeats = values.shape[1] // cos_ref.shape[1]
        cosine = jnp.concatenate([cos_ref[...]] * repeats, axis=1)
        sine = jnp.concatenate([sin_ref[...]] * repeats, axis=1)
        return values * cosine + swap_halves(values) * sine

    @pl.when(step == 0)
    def _():
        out_ref[...] = (turn(before) * HEAD_DIMENSION ** (-0.5)).astype(BF16)

    @pl.when(step == 1)
    def _():
        out_ref[:, :key_width] = turn(before[:, :key_width]).astype(BF16)
        out_ref[:, key_width:] = before[:, key_width:].astype(BF16)


def project(x, gain, weight, cosine, sine, query_width, key_width):
    rows, width = x.shape
    total = weight.shape[1]
    tile = query_width
    assert total == 2 * tile
    whole = lambda shape: pl.BlockSpec(shape, lambda i: (0, 0))
    return pl.pallas_call(
        lambda *refs: project_kernel(key_width, *refs),
        grid=(2,),
        out_shape=(
            jax.ShapeDtypeStruct((rows, total), BF16),
            jax.ShapeDtypeStruct((rows, width), BF16),
        ),
        in_specs=[
            whole((rows, width)),
            whole((1, width)),
            pl.BlockSpec((width, tile), lambda i: (0, i)),
            whole(cosine.shape),
            whole(sine.shape),
        ],
        out_specs=(pl.BlockSpec((rows, tile), lambda i: (0, i)), whole((rows, width))),
        compiler_params=pltpu.CompilerParams(vmem_limit_bytes=VMEM_LIMIT),
        cost_estimate=lasting(8.6),
        name="project_heads",
    )(x, gain, weight, cosine, sine)


def pair_of(block, which):
    values = block.astype(F32)
    low = lax.broadcasted_iota(jnp.int32, values.shape, 1) < HEAD_DIMENSION
    other = pltpu.roll(values, HEAD_DIMENSION, 1)
    return jnp.where(low, *((values, other) if which == 0 else (other, values))).astype(BF16)


def head_of(block, which):
    low = lax.broadcasted_iota(jnp.int32, block.shape, 1) < HEAD_DIMENSION
    return jnp.where(low if which == 0 else ~low, block.astype(F32), 0.0).astype(BF16)


def fill_bias(bias_ref, begin_ref):
    key = lax.broadcasted_iota(jnp.int32, bias_ref.shape, 0)
    query = lax.broadcasted_iota(jnp.int32, bias_ref.shape, 1)
    bias_ref[...] = jnp.where((key <= query) & (key >= begin_ref[...]), 0.0, -1e30)


def attend_kernel(tile, q_ref, k_ref, v_ref, begin_ref, out_ref, lse_ref, bias_ref):
    rows = q_ref.shape[0]
    lanes = 2 * HEAD_DIMENSION

    @pl.when(pl.program_id(0) == 0)
    def _():
        fill_bias(bias_ref, begin_ref)

    for c in range(2):
        place = slice(c * lanes, (c + 1) * lanes)
        keys = pair_of(k_ref[...], c)
        values = pair_of(v_ref[...], c)
        for start in range(0, rows, tile):
            span = slice(start, start + tile)
            reach = start + tile
            query = q_ref[span, place]
            outs = []
            for h in range(2):
                scores = lax.dot_general(
                    keys[:reach], head_of(query, h), NT, preferred_element_type=F32
                )
                scores = scores + bias_ref[:reach, span]
                peak = jnp.max(scores, axis=0, keepdims=True)
                raised = jnp.exp(scores - peak)
                total = jnp.sum(raised, axis=0, keepdims=True)
                mixed = lax.dot_general(
                    values[:reach], raised.astype(BF16), TN, preferred_element_type=F32
                )
                part = slice(h * HEAD_DIMENSION, (h + 1) * HEAD_DIMENSION)
                outs.append(mixed[part] * (1.0 / total))
                lse_ref[0, 2 * c + h : 2 * c + h + 1, span] = peak + jnp.log(total)
            out_ref[span, place] = jnp.concatenate(outs, axis=0).T.astype(BF16)


def attend(qkv, begin, query_width, key_width):
    rows = qkv.shape[0]
    lanes = 2 * HEAD_DIMENSION
    key_start = query_width // lanes
    value_start = (query_width + key_width) // lanes
    steps = key_width // lanes
    pair = pl.BlockSpec((rows, 2 * lanes), lambda i: (0, i))
    return pl.pallas_call(
        lambda *refs: attend_kernel(min(128, rows), *refs),
        grid=(steps,),
        out_shape=(
            jax.ShapeDtypeStruct((rows, query_width), BF16),
            jax.ShapeDtypeStruct((steps, 4, rows), F32),
        ),
        in_specs=[
            pair,
            pl.BlockSpec((rows, lanes), lambda i: (0, key_start + i)),
            pl.BlockSpec((rows, lanes), lambda i: (0, value_start + i)),
            pl.BlockSpec(begin.shape, lambda i: (0, 0)),
        ],
        out_specs=(pair, pl.BlockSpec((1, 4, rows), lambda i: (i, 0, 0))),
        scratch_shapes=[pltpu.VMEM((rows, rows), F32)],
        compiler_params=pltpu.CompilerParams(vmem_limit_bytes=VMEM_LIMIT),
        cost_estimate=lasting(11.5),
        name="attend",
    )(qkv, qkv, qkv, begin)


def attend_back_kernel(
    tile, q_ref, k_ref, v_ref, grad_ref, lse_ref, begin_ref, cos_ref, sin_ref,
    dq_ref, dk_ref, dv_ref, bias_ref, dk_sum, dv_sum,
):
    rows = q_ref.shape[0]
    lanes = 2 * HEAD_DIMENSION

    @pl.when(pl.program_id(0) == 0)
    def _():
        fill_bias(bias_ref, begin_ref)

    def turn_back(values, cosine, sine):
        return values * cosine - swap_halves(values) * sine

    for c in range(2):
        place = slice(c * lanes, (c + 1) * lanes)
        keys = pair_of(k_ref[...], c)
        values = pair_of(v_ref[...], c)
        for start in reversed(range(0, rows, tile)):
            span = slice(start, start + tile)
            reach = start + tile
            outs = []
            dk = dv = None
            for h in range(2):
                query = head_of(q_ref[span, place], h)
                grad = head_of(grad_ref[span, place], h)
                scores = lax.dot_general(keys[:reach], query, NT, preferred_element_type=F32)
                row = lse_ref[0, 2 * c + h : 2 * c + h + 1, span]
                probs = jnp.exp(scores + bias_ref[:reach, span] - row)
                grad_probs = lax.dot_general(values[:reach], grad, NT, preferred_element_type=F32)
                delta = jnp.sum(probs * grad_probs, axis=0, keepdims=True)
                grad_scores = (probs * (grad_probs - delta)).astype(BF16)
                turned = lax.dot_general(keys[:reach], grad_scores, TN, preferred_element_type=F32)
                outs.append(turned[h * HEAD_DIMENSION : (h + 1) * HEAD_DIMENSION])
                dk_part = jnp.dot(grad_scores, query, preferred_element_type=F32)
                dv_part = jnp.dot(probs.astype(BF16), grad, preferred_element_type=F32)
                dk = dk_part if dk is None else dk + dk_part
                dv = dv_part if dv is None else dv + dv_part
            if reach == rows:
                dk_sum[c] = dk
                dv_sum[c] = dv
            else:
                dk_sum[c, :reach, :] += dk
                dv_sum[c, :reach, :] += dv
            dq = turn_back(jnp.concatenate(outs, axis=0).T, cos_ref[span, :], sin_ref[span, :])
            dq_ref[span, place] = (dq * HEAD_DIMENSION ** (-0.5)).astype(BF16)
    low = lax.broadcasted_iota(jnp.int32, (rows, lanes), 1) < HEAD_DIMENSION

    def both(sums):
        return jnp.where(
            low, *(sums[c] + pltpu.roll(sums[c], HEAD_DIMENSION, 1) for c in range(2))
        )

    dk_ref[...] = turn_back(both(dk_sum), cos_ref[...], sin_ref[...]).astype(BF16)
    dv_ref[...] = both(dv_sum).astype(BF16)


def attend_back(qkv, grad, lse, begin, cosine, sine, query_width, key_width, first, count):
    rows = qkv.shape[0]
    lanes = 2 * HEAD_DIMENSION
    key_start = query_width // lanes + first
    value_start = (query_width + key_width) // lanes + first
    pair = pl.BlockSpec((rows, 2 * lanes), lambda i: (0, first + i))
    whole = lambda shape: pl.BlockSpec(shape, lambda i: (0, 0))
    return pl.pallas_call(
        lambda *refs: attend_back_kernel(min(256, rows), *refs),
        grid=(count,),
        out_shape=(
            jax.ShapeDtypeStruct((rows, 2 * lanes * count), BF16),
            jax.ShapeDtypeStruct((rows, lanes * count), BF16),
            jax.ShapeDtypeStruct((rows, lanes * count), BF16),
        ),
        in_specs=[
            pair,
            pl.BlockSpec((rows, lanes), lambda i: (0, key_start + i)),
            pl.BlockSpec((rows, lanes), lambda i: (0, value_start + i)),
            pair,
            pl.BlockSpec((1, 4, rows), lambda i: (first + i, 0, 0)),
            whole(begin.shape),
            whole(cosine.shape),
            whole(sine.shape),
        ],
        out_specs=(
            pl.BlockSpec((rows, 2 * lanes), lambda i: (0, i)),
            pl.BlockSpec((rows, lanes), lambda i: (0, i)),
            pl.BlockSpec((rows, lanes), lambda i: (0, i)),
        ),
        scratch_shapes=[
            pltpu.VMEM((rows, rows), F32),
            pltpu.VMEM((2, rows, lanes), F32),
            pltpu.VMEM((2, rows, lanes), F32),
        ],
        compiler_params=pltpu.CompilerParams(vmem_limit_bytes=VMEM_LIMIT),
        cost_estimate=lasting(5.1 * count),
        name="attend_back",
    )(qkv, qkv, qkv, grad, lse, begin, cosine, sine)


def local(
    tokens,
    lengths,
    routes,
    cotangent,
    gain_attn,
    w_query,
    key_projection_weight,
    value_projection_weight,
    w_out,
    gain_moe,
    w_router,
    w_gate,
    w_up,
    w_down,
):
    count_of_rows, model_width = tokens.shape
    expert_count = lax.axis_size("expert")
    devices = lax.axis_size("dp")
    e_index = lax.axis_index("expert")
    top_count = routes.shape[1]
    capacity = 2 * count_of_rows * top_count // expert_count
    shard_rows = gain_attn.shape[0]
    query_width = w_query.shape[1]
    key_width = key_projection_weight.shape[1]

    lanes = -(-(expert_count + 2) // 128) * 128
    small = jnp.concatenate(
        [
            w_router,
            gain_attn[:, None],
            gain_moe[:, None],
            jnp.zeros((shard_rows, lanes - expert_count - 2), BF16),
        ],
        axis=1,
    )
    routes_rel = gather_small(routes.T)
    (qkv_w, out_w, small_w), cot_blocks, _ = gather_weights(
        [w_query, key_projection_weight, value_projection_weight, w_out, small],
        (query_width + 2 * key_width, model_width, lanes),
        cotangent,
    )
    router_w = small_w[:, :expert_count]
    gains = small_w[:, expert_count : expert_count + 2].astype(F32).T
    gain_first, gain_second = gains[0], gains[1]

    index_rows = jnp.arange(count_of_rows, dtype=jnp.int32)
    before = (index_rows[:, None] < index_rows[None, :]).astype(BF16)

    def slots_of(expert):
        hit = jnp.any(routes_rel == expert, axis=1)
        place = jnp.dot(hit.astype(BF16), before, preferred_element_type=F32)
        return jnp.where(hit, place.astype(jnp.int32), -1)

    slots_mine = slots_of(e_index)
    slots_sibling = slots_of(e_index ^ 1)
    mine_row = (jnp.arange(lanes) == e_index).astype(F32)[None]
    gate_up_w = jnp.concatenate([w_gate[0], w_up[0]], axis=1)
    down_w = w_down[0]

    _, position = positions_of(lengths[0], count_of_rows)
    begin = (index_rows - position)[None]
    half = HEAD_DIMENSION // 2
    cosine, sine = rope_tables(position, HEAD_DIMENSION)
    cosine = jnp.concatenate([cosine] * 4, axis=1)
    sine = jnp.concatenate([-sine, sine] * 2, axis=1)

    qkv, first_normalized = project(
        tokens, gain_first[None], qkv_w, cosine, sine, query_width, key_width
    )
    attn_rows, lse = attend(qkv, begin, query_width, key_width)
    resid_in = tokens.astype(F32)
    resid_mid = resid_in + jnp.dot(attn_rows, out_w, preferred_element_type=F32)
    inverse_two = lax.rsqrt(jnp.mean(resid_mid * resid_mid, axis=-1, keepdims=True) + eps_norm)
    normed_two = (resid_mid * inverse_two * gain_second).astype(BF16)

    cot_list = [cot_blocks[m] for m in range(expert_count)]
    tok_blocks = {}

    logits = jnp.dot(normed_two, router_w, preferred_element_type=F32)
    expert_ids = jnp.arange(expert_count, dtype=jnp.int32)
    chosen = (routes[:, :, None] == expert_ids[None, None, :]).astype(F32)
    picked = jnp.sum(logits[:, None, :] * chosen, axis=-1)
    gates = jax.nn.softmax(picked, axis=-1)

    def run_group(low_mask):
        pair = (low_mask, low_mask ^ 1)
        return expert_group(
            [tok_blocks[m] for m in pair],
            [cot_blocks[m] for m in pair],
            slots_mine[low_mask : low_mask + 2],
            routes_rel[low_mask : low_mask + 2],
            mine_row,
            small_w,
            gate_up_w,
            down_w,
            capacity,
        )

    sent = after(normed_two, slots_mine, slots_sibling, *cot_list)
    tok_blocks[0] = sent
    tok_blocks[1] = hop(sent, "expert", 1)
    results = {0: run_group(0)}
    tok_blocks.update(gather_links(sent, lambda pair: after_all(pair, results[0][2])))
    for m in range(2, expert_count, 2):
        tok_blocks[m ^ 1] = hop(tok_blocks[m], "expert", 1)
    last_mask = expert_count - 2
    in_partial, pending, direct = {}, {}, None

    def return_rows(low_mask, *earlier):
        keep_in, give_in = results[low_mask][2:4]
        slots = pending[low_mask][2]
        arrived = hop(give_in, "expert", 1)
        if earlier:
            keep_in = after(keep_in, *earlier)
        in_partial[low_mask] = combine([keep_in, arrived], [slots])[0]

    for low_mask in range(0, expert_count, 2):
        if low_mask:
            if expert_count == 8:
                earlier = [results[low_mask - 2][2]]
                if low_mask == last_mask:
                    return_rows(2)
                    return_rows(4)
                    direct_rows = return_direct(in_partial)
                    direct = mixed_hop(direct_rows, 2, 4)
                    earlier.append(direct_rows)
                tok_blocks[low_mask] = after(tok_blocks[low_mask], *earlier)
            results[low_mask] = run_group(low_mask)
        keep_moe, give_moe = results[low_mask][:2]
        slots = jnp.stack([slots_mine[low_mask], slots_sibling[low_mask]])
        pending[low_mask] = (keep_moe, give_moe, slots)
    return_rows(last_mask, *([] if direct is None else [direct]))
    if expert_count == 8:
        return_rows(0, in_partial[last_mask])
    else:
        for low_mask in range(0, last_mask, 2):
            return_rows(low_mask)
    saved = [list(results[low_mask][4:8]) for low_mask in range(0, expert_count, 2)]
    saved[0][0] = after(saved[0][0], in_partial[last_mask])
    expert_grads = expert_wgrad(*[list(part) for part in zip(*saved)])
    if direct is None:
        grad_terms = return_halving(in_partial)
        passed = grad_terms[0]
    else:
        passed = after(return_passed(in_partial), expert_grads)
        onward = return_onward(in_partial, passed)
        grad_terms = [in_partial[0], direct, mixed_hop(onward, 4, 2)]
    expert_pieces = lax.psum_scatter(
        after(expert_grads, passed).reshape(-1, model_width), "dp", scatter_dimension=0, tiled=True
    ).astype(F32)

    gives = [
        hop(after(pending[low_mask][1], passed), "expert", 1)
        for low_mask in range(0, expert_count, 2)
    ]
    moe_rows, moe_slots = [], []
    for arrived, (keep_moe, _, slots) in zip(gives, pending.values()):
        moe_rows += [keep_moe, arrived]
        moe_slots.append(slots)
    if expert_count == 8:
        moe_list = combine(moe_rows, moe_slots)
        grad_terms = after_all(grad_terms, *moe_list)
    else:
        moe_list = [
            combine(moe_rows[2 * i : 2 * i + 2], moe_slots[i : i + 1])[0]
            for i in range(len(moe_slots))
        ]
    moe_partial = dict(zip(pending, moe_list))

    grad_final = cotangent.astype(F32)
    returned = sum_terms(grad_terms)
    gate_columns = returned[:, model_width : model_width + expert_count]
    gate_columns += returned[:, model_width + lanes // 2 :][:, :expert_count]
    grad_gates = jnp.sum(gate_columns[:, None, :] * chosen, axis=-1)
    grad_picked = gates * (grad_gates - jnp.sum(gates * grad_gates, axis=-1, keepdims=True))
    grad_logits = jnp.sum(grad_picked[:, :, None] * chosen, axis=1).astype(BF16)
    grad_normed_two = jnp.dot(grad_logits, router_w.T, preferred_element_type=F32)
    grad_normed_two = grad_normed_two + returned[:, :model_width]
    scaled_two = grad_normed_two * gain_second
    gain_terms = (grad_normed_two * resid_mid * inverse_two).astype(BF16)
    grad_mid = (
        grad_final
        + inverse_two * scaled_two
        - resid_mid
        * inverse_two
        * inverse_two
        * inverse_two
        * jnp.mean(resid_mid * scaled_two, axis=-1, keepdims=True)
    )
    grad_mid_low = grad_mid.astype(BF16)
    grad_attn = lax.dot_general(grad_mid_low, out_w, NT, preferred_element_type=F32).astype(BF16)

    pairs = key_width // (2 * HEAD_DIMENSION)
    cut = pairs // 2
    def back(grad, first, count):
        return attend_back(
            qkv, grad, lse, begin, cosine, sine, query_width, key_width, first, count
        )

    parts = [back(grad_attn, 0, cut)]
    if direct is None:
        moe_terms = return_halving(moe_partial)
        moe_first, moe_last = moe_terms, moe_terms[0]
    else:
        for m in (2, 4, 6):
            moe_partial[m] = after(moe_partial[m], grad_terms[-1])
        moe_first = return_onward(
            moe_partial, after(return_passed(moe_partial), parts[0][0])
        )
        direct_rows = after(return_direct(moe_partial), parts[0][0])
        moe_last = mixed_hop(moe_first, 4, 2)
        moe_terms = [
            moe_partial[0],
            mixed_hop(after(direct_rows, moe_last), 2, 4),
            moe_last,
        ]
        moe_first = (moe_first, direct_rows)
    logits_wide = jnp.pad(grad_logits, ((0, 0), (0, lanes - expert_count)))
    gain_column = jnp.broadcast_to(jnp.arange(lanes) == expert_count, logits_wide.shape)
    early_send, finish_early = reduce_grads(
        [[(first_normalized, after(part, *moe_first))] for part in parts[0]]
        + [
            [(attn_rows, grad_mid_low)],
            [(normed_two, logits_wide), (gain_terms, gain_column.astype(BF16))],
        ]
    )
    parts.append(back(after(grad_attn, early_send, moe_last), cut, pairs - cut))
    resid_late, *moe_terms = after_all([resid_mid, *moe_terms], parts[1][0])
    mixed_out = (resid_late + sum_terms(moe_terms)).astype(BF16)
    early_near = finish_early[0](
        lambda values: after(values, parts[1][0], moe_terms[1 % len(moe_terms)]), moe_last
    )
    late_send, finish_late = reduce_grads(
        [[(first_normalized, after(part, early_near))] for part in parts[1]]
    )
    grad_qkv = jnp.concatenate(
        [after(part[i], late_send) for i in range(3) for part in parts], axis=1
    )
    grad_normed_one = lax.dot_general(grad_qkv, qkv_w, NT, preferred_element_type=F32)
    inverse_one = lax.rsqrt(jnp.mean(resid_in * resid_in, axis=-1, keepdims=True) + eps_norm)
    scaled_one = grad_normed_one * gain_first
    grad_input = (
        grad_mid
        + inverse_one * scaled_one
        - resid_in
        * inverse_one
        * inverse_one
        * inverse_one
        * jnp.mean(resid_in * scaled_one, axis=-1, keepdims=True)
    )
    gate_rows = model_width // devices
    hidden = down_w.shape[0]
    grad_input = grad_input.astype(BF16)
    early_line = finish_early[1](early_near, lambda pieces: after_all(pieces, grad_input))
    late_near = finish_late[0](lambda values: after(values, early_line))
    late_line = finish_late[1](late_near, lambda pieces: pieces)
    reduced = reduce_dp(jnp.concatenate([early_line, late_line], axis=-1), model_width)
    widths = [part.shape[1] for part in parts[0]] + [model_width, lanes]
    widths += [part.shape[1] for part in parts[1]]
    starts = [sum(widths[:i]) for i in range(len(widths))]
    pieces = [reduced[:, s : s + w].astype(F32) for s, w in zip(starts, widths)]
    grad_out_part, small_part = pieces[3:5]
    columns = [jnp.concatenate([pieces[i], pieces[5 + i]], axis=1) for i in range(3)]
    projections = (w_query, key_projection_weight, value_projection_weight)
    grad_gain_one = sum(
        jnp.sum(weight.astype(F32) * grad, axis=1) for weight, grad in zip(projections, columns)
    ) / gain_attn.astype(F32)
    return (
        mixed_out,
        grad_input,
        grad_gain_one,
        *columns,
        grad_out_part,
        small_part[:, expert_count],
        small_part[:, :expert_count],
        expert_pieces[None, :gate_rows, :hidden],
        expert_pieces[None, :gate_rows, hidden:],
        expert_pieces[None, gate_rows:, :],
    )


def solution(mesh):
    placed = (
        P(("dp", "expert"), None),
        P(("dp", "expert"), None),
        P(("dp", "expert"), None),
        P(("dp", "expert"), None),
        P("dp"),
        P("dp", None),
        P("dp", None),
        P("dp", None),
        P("dp", None),
        P("dp"),
        P("dp", None),
        P("expert", None, None),
        P("expert", None, None),
        P("expert", None, None),
    )
    return jax.shard_map(
        local,
        mesh=mesh,
        in_specs=placed,
        out_specs=(
            P(("dp", "expert"), None),
            P(("dp", "expert"), None),
            P("dp"),
            P("dp", None),
            P("dp", None),
            P("dp", None),
            P("dp", None),
            P("dp"),
            P("dp", None),
            P("expert", "dp", None),
            P("expert", "dp", None),
            P("expert", "dp", None),
        ),
        check_vma=False,
    )
```

```python
import math

import jax
import jax.numpy as jnp
from jax import lax
from jax.experimental import pallas as pl
from jax.experimental.pallas import tpu as pltpu
from jax.sharding import PartitionSpec as P

QUERY_HEADS = 16
KEY_VALUE_HEADS = 8
HEAD_DIMENSION = 64


eps_norm = 1e-06


def positions_of(lengths_row, count_of_rows):
    index_rows = jnp.arange(count_of_rows, dtype=jnp.int32)
    ends = jnp.cumsum(lengths_row)
    member = jnp.sum((index_rows[:, None] >= ends[None, :]).astype(jnp.int32), axis=1)
    starts = ends - lengths_row
    onehot = member[:, None] == jnp.arange(lengths_row.shape[0], dtype=jnp.int32)[None, :]
    begin = jnp.sum(jnp.where(onehot, starts[None, :], 0), axis=1)
    return (member, index_rows - begin)


def rope_tables(positions, head_size):
    half_size = head_size // 2
    freq = jnp.exp(
        jnp.arange(half_size, dtype=jnp.float32) * (-2.0 * math.log(10000.0) / head_size)
    )
    angle = positions.astype(jnp.float32)[:, None] * freq[None, :]
    return (jnp.cos(angle), jnp.sin(angle))


F32 = jnp.float32
BF16 = jnp.bfloat16
VMEM_LIMIT = 56 * 1024 * 1024
NT = (((1,), (1,)), ((), ()))
TN = (((0,), (0,)), ((), ()))


def lasting(microseconds):
    return pl.CostEstimate(
        flops=int(microseconds * 1.15e9), bytes_accessed=1 << 20, transcendentals=0
    )


def hop(values, axis, mask):
    count = lax.axis_size(axis)
    return lax.ppermute(values, axis, [(i, i ^ mask) for i in range(count)])


def after_all(values, *earlier):
    return list(lax.optimization_barrier((*values, *earlier))[: len(values)])


def link_bits(count):
    return [1 << i for i in range(1, count.bit_length() - 1)]


def after(values, *earlier):
    return lax.optimization_barrier((values, *earlier))[0]


def mixed_hop(values, first, second):
    count = lax.axis_size("expert")
    return lax.ppermute(
        values, "expert", [(i, i ^ (second if i % 2 else first)) for i in range(count)]
    )


def gather_links(block, hold=lambda pair: pair):
    count = lax.axis_size("expert")
    blocks = {0: block}
    if count == 8:
        blocks[2], blocks[4] = hold((hop(block, "expert", 2), hop(block, "expert", 4)))
        parity = lax.axis_index("expert") % 2
        blocks[6] = mixed_hop(jnp.where(parity == 0, blocks[2], blocks[4]), 4, 2)
        return blocks
    for bit in link_bits(count):
        for m in list(blocks):
            blocks[m ^ bit] = hop(blocks[m], "expert", bit)
    return blocks


def gather_plane(block):
    blocks = gather_links(block)
    for m in list(blocks):
        blocks[m ^ 1] = hop(blocks[m], "expert", 1)
    return blocks


def gather_small(values):
    count = lax.axis_size("expert")
    rows = values[None]
    bit = 1
    while bit < count:
        rows = jnp.concatenate([rows, hop(rows, "expert", bit)], axis=0)
        bit *= 2
    return rows


def place_kernel(devices, rows, *refs):
    near, own_ref, outs = refs[:-4], refs[-4], refs[-3:]
    z_index = lax.axis_index("dp")
    e_index = lax.axis_index("expert")
    shard_rows = own_ref.shape[0]

    def put(at, count, values):
        column = 0
        for out in outs:
            width = out.shape[1]
            out[pl.ds(pl.multiple_of(at, 16), count), :] = values[:, column : column + width]
            column += width

    put(z_index * shard_rows, shard_rows, own_ref[...])
    for m, block in enumerate(near):
        for zm in range(1, devices):
            at = (z_index ^ zm) * shard_rows + (e_index ^ m) * rows
            put(at, rows, block[(zm - 1) * rows : zm * rows, :])


def gather_weights(shards, widths, cotangent):
    devices = lax.axis_size("dp")
    count = lax.axis_size("expert")
    shard_rows = shards[0].shape[0]
    rows = shard_rows // count
    if rows % 16 or count != 8:
        whole = lax.all_gather(jnp.concatenate(shards, axis=1), "dp", axis=0, tiled=True)
        starts = [sum(widths[:i]) for i in range(len(widths))]
        arrays = [whole[:, s : s + w] for s, w in zip(starts, widths)]
        return arrays, gather_plane(cotangent), whole
    start = lax.axis_index("expert") * rows
    mine = jnp.concatenate(
        [lax.dynamic_slice_in_dim(shard, start, rows, 0) for shard in shards], axis=1
    )
    far = jnp.concatenate([hop(mine, "dp", m) for m in range(1, devices)], axis=0)
    cotangent = after(cotangent, mine)
    cot = {0: cotangent, 2: hop(cotangent, "expert", 2), 4: hop(cotangent, "expert", 4)}
    far = after(far, cot[2], cot[4])
    near = gather_links(far)
    for m in (0, 2, 4):
        near[m ^ 1] = hop(near[m], "expert", 1)
    near[7] = hop(after(near[6], near[1], near[3], near[5]), "expert", 1)
    parity = lax.axis_index("expert") % 2
    cot[6] = mixed_hop(after(jnp.where(parity == 0, cot[2], cot[4]), near[6]), 4, 2)
    for m in list(cot):
        cot[m ^ 1] = hop(after(cot[m], near[7]), "expert", 1)
    vmem = pl.BlockSpec(memory_space=pltpu.VMEM)
    arrays = pl.pallas_call(
        lambda *refs: place_kernel(devices, rows, *refs),
        out_shape=[
            jax.ShapeDtypeStruct((shard_rows * devices, width), mine.dtype) for width in widths
        ],
        in_specs=[vmem] * (count + 1),
        out_specs=[vmem] * len(widths),
        compiler_params=pltpu.CompilerParams(vmem_limit_bytes=VMEM_LIMIT),
        cost_estimate=lasting(6.0),
        name="place_weights",
    )(*[near[m] for m in range(count)], jnp.concatenate(shards, axis=1))
    return arrays, cot, near[7]


def split_kernel(columns, *refs):
    keep_ref, send_ref = refs[-2:]
    core = lax.axis_index("expert") % 2
    rows = keep_ref.shape[0] * 2
    group = rows // (lax.axis_size("dp") * lax.axis_size("expert"))
    start = at = 0
    for width, terms in columns:
        total = None
        for _ in range(terms):
            part = lax.dot_general(
                refs[at][...], refs[at + 1][...], TN, preferred_element_type=F32
            )
            total = part if total is None else total + part
            at += 2
        low = total.astype(BF16)
        place = slice(start, start + width)
        start += width
        for who, (even, odd) in enumerate(((keep_ref, send_ref), (send_ref, keep_ref))):

            @pl.when(core == who)
            def _(even=even, odd=odd, low=low, place=place):
                for i in range(rows // group):
                    out = odd if i % 2 else even
                    out[i // 2 * group : (i // 2 + 1) * group, place] = low[
                        i * group : (i + 1) * group, :
                    ]


def split_grads(columns):
    height = columns[0][0][0].shape[1]
    widths = [terms[0][1].shape[1] for terms in columns]
    width = sum(widths)
    vmem = pl.BlockSpec(memory_space=pltpu.VMEM)
    operands = [array for terms in columns for pair in terms for array in pair]
    shape = tuple((w, len(terms)) for w, terms in zip(widths, columns))
    return pl.pallas_call(
        lambda *refs: split_kernel(shape, *refs),
        out_shape=(jax.ShapeDtypeStruct((height // 2, width), BF16),) * 2,
        in_specs=[vmem] * len(operands),
        out_specs=(vmem, vmem),
        compiler_params=pltpu.CompilerParams(vmem_limit_bytes=VMEM_LIMIT),
        cost_estimate=lasting(1.0 + 5.0 * width / height),
        name="weight_grads",
    )(*operands)


def pick(values, index, axis):
    return lax.dynamic_index_in_dim(values, index, axis, keepdims=False)


def join_cores(keep, arrived, hold=lambda values: values):
    near = hold(keep.astype(F32) + arrived.astype(F32)).astype(BF16)
    devices, chips = lax.axis_size("dp"), lax.axis_size("expert") // 2
    return near.reshape(devices, chips, -1, near.shape[-1])


def across_cores(keep, send, hold=lambda values: values):
    return join_cores(keep, hop(send, "expert", 1), hold)


def across_links(near, hold=lambda pieces: pieces):
    chip = lax.axis_index("expert") // 2
    pieces = [
        hop(pick(near, chip ^ m, 1), "expert", 2 * m).astype(F32) for m in range(1, near.shape[1])
    ]
    line = pick(near, chip, 1).astype(F32)
    for piece in hold(pieces):
        line = line + piece
    return line.astype(BF16)


def across_links_start(near, hold):
    chip, across = lax.axis_index("expert") // 2, near.shape[1] - 1
    pieces = [
        hop(pick(near, chip ^ m, 1), "expert", 2 * m) for m in range(1, across + 1)
    ]
    line = pick(near, chip, 1).astype(F32)
    for piece in hold(pieces[:-1]):
        line = line + piece.astype(F32)
    return line, pieces[-1]


def across_dp(line, hold=lambda pieces: pieces):
    z_index = lax.axis_index("dp")
    pieces = [hop(pick(line, z_index ^ m, 0), "dp", m) for m in range(1, line.shape[0])]
    done = pick(line, z_index, 0).astype(F32)
    for piece in hold(pieces):
        done = done + piece.astype(F32)
    return done.astype(BF16)


def pick_rows(slots, capacity):
    index = lax.broadcasted_iota(jnp.int32, (capacity, slots.shape[1]), 0)
    return index == slots


def expert_kernel(capacity, blocks, *refs):
    tok_hbm, cot_hbm = refs[:blocks], refs[blocks : 2 * blocks]
    slot_ref, route_ref, mine_ref, *weights_hbm = refs[2 * blocks : 2 * blocks + 6]
    refs = refs[2 * blocks + 6 :]
    count = 2 * blocks + 4
    outs, refs = refs[:count], refs[count:]
    tok, cot, refs = refs[:blocks], refs[blocks : 2 * blocks], refs[2 * blocks :]
    weights, stores = refs[:3], refs[3 : 3 + count]
    chosen_ref, sems = refs[3 + count :]
    router_ref, gate_up_ref, down_ref = weights
    rows_ref, ge_ref, hid_ref, dgu_ref = stores[2 * blocks :]
    pairs = [pair for i in range(blocks) for pair in ((tok_hbm[i], tok[i]), (cot_hbm[i], cot[i]))]
    pairs[2:2] = list(zip(weights_hbm, weights))
    loads = [
        pltpu.make_async_copy(source, target, sems.at[i])
        for i, (source, target) in enumerate(pairs)
    ]
    for load in loads:
        load.start()
    writes = []

    def write(index, place=None):
        source, target = stores[index], outs[index]
        if place is not None:
            source, target = source.at[place, :], target.at[place, :]
        copy = pltpu.make_async_copy(source, target, sems.at[len(loads) + len(writes)])
        copy.start()
        writes.append(copy)

    tokens = tok[0].shape[0]
    lanes = mine_ref.shape[1]
    top = route_ref.shape[1]
    hidden_width = hid_ref.shape[1]
    for b in range(blocks):
        place = pl.ds(b * capacity, capacity)
        loads[3 + 2 * b if b else 0].wait()
        picked = pick_rows(slot_ref[b : b + 1, :], capacity)
        sel = picked.astype(F32).astype(BF16)
        rows = jnp.dot(sel, tok[b][...], preferred_element_type=F32).astype(BF16)
        rows_ref[place, :] = rows
        write(2 * blocks, place)
        loads[4 + 2 * b if b else 1].wait()
        drows = jnp.dot(sel, cot[b][...], preferred_element_type=F32)
        expert = lax.broadcasted_iota(jnp.int32, (lanes, tokens), 0)
        named = route_ref[b, 0:1, :] == expert
        for k in range(1, top):
            named = named | (route_ref[b, k : k + 1, :] == expert)
        chosen_ref[...] = lax.dot_general(
            sel, named.astype(F32).astype(BF16), NT, preferred_element_type=F32
        )
        if b == 0:
            loads[2].wait()
        logits = jnp.dot(rows, router_ref[...], preferred_element_type=F32)
        chosen = chosen_ref[...] > 0.5
        shown = jnp.where(chosen, logits, -1e30)
        weight = jnp.where(chosen, jnp.exp(shown - jnp.max(shown, axis=-1, keepdims=True)), 0.0)
        total = jnp.sum(weight, axis=-1, keepdims=True)
        gate = jnp.sum(weight * mine_ref[...], axis=-1, keepdims=True) / jnp.where(
            total > 0.0, total, 1.0
        )
        grad_out = (gate * drows).astype(BF16)
        ge_ref[place, :] = grad_out
        write(2 * blocks + 1, place)
        if b == 0:
            loads[3].wait()
        gate_up = jnp.dot(rows, gate_up_ref[...], preferred_element_type=F32)
        gate_pre = gate_up[:, :hidden_width]
        up_pre = gate_up[:, hidden_width:]
        if b == 0:
            loads[4].wait()
        grad_hidden = lax.dot_general(grad_out, down_ref[...], NT, preferred_element_type=F32)
        sigm = 1.0 / (1.0 + jnp.exp(-gate_pre))
        activated = gate_pre * sigm
        hidden = (activated * up_pre).astype(BF16)
        hid_ref[place, :] = hidden
        write(2 * blocks + 2, place)
        dgate = (grad_hidden * up_pre * sigm * (1.0 + gate_pre * (1.0 - sigm))).astype(BF16)
        dup = (grad_hidden * activated).astype(BF16)
        dgu_ref[place, :hidden_width] = dgate
        dgu_ref[place, hidden_width:] = dup
        write(2 * blocks + 3, place)
        back = stores[blocks + b]
        width = rows.shape[1]
        back[:, :width] = lax.dot_general(
            dgu_ref[place, :], gate_up_ref[...], NT, preferred_element_type=F32
        ).astype(BF16)
        result = jnp.dot(hidden, down_ref[...], preferred_element_type=F32)
        result = result.astype(BF16).astype(F32)
        moe = stores[b]
        moe[...] = (gate * result).astype(BF16)
        write(b)
        gate_grad = jnp.sum(drows * result, axis=-1, keepdims=True)
        high = gate_grad.astype(BF16).astype(F32)
        mine = mine_ref[...]
        back[:, width:] = (
            high * mine + (gate_grad - high) * pltpu.roll(mine, lanes // 2, 1)
        ).astype(BF16)
        write(blocks + b)
    for copy in writes:
        copy.wait()


def expert_group(tok, cot, slots, routes, mine, router, gate_up, down, capacity):
    blocks = len(tok)
    width = tok[0].shape[1]
    hidden = down.shape[0]
    tokens = slots.shape[1]
    rows = blocks * capacity
    vmem = pl.BlockSpec(memory_space=pltpu.VMEM)
    far = pl.BlockSpec(memory_space=pl.ANY)
    wide = width + mine.shape[1]
    shapes = [(capacity, width)] * blocks + [(capacity, wide)] * blocks
    shapes += [(rows, width), (rows, width), (rows, hidden)]
    shapes.append((rows, 2 * hidden))
    return pl.pallas_call(
        lambda *refs: expert_kernel(capacity, blocks, *refs),
        out_shape=[jax.ShapeDtypeStruct(shape, BF16) for shape in shapes],
        in_specs=[far] * (2 * blocks) + [vmem] * 3 + [far] * 3,
        out_specs=[far] * len(shapes),
        scratch_shapes=[pltpu.VMEM((tokens, width), BF16)] * (2 * blocks)
        + [pltpu.VMEM(array.shape, BF16) for array in (router, gate_up, down)]
        + [pltpu.VMEM(shape, BF16) for shape in shapes]
        + [
            pltpu.VMEM((capacity, mine.shape[1]), F32),
            pltpu.SemaphoreType.DMA((2 * blocks + 3 + 6 * blocks,)),
        ],
        compiler_params=pltpu.CompilerParams(vmem_limit_bytes=VMEM_LIMIT),
        cost_estimate=lasting(2.5 + 4.0 * blocks),
        name="expert_group",
    )(*tok, *cot, slots, routes, mine, router, gate_up, down)


def combine_kernel(capacity, blocks, *refs):
    slot_refs = refs[2 * blocks : 3 * blocks]
    outs = refs[3 * blocks :]
    for i in range(blocks):
        total = None
        for who, rows in enumerate(refs[2 * i : 2 * i + 2]):
            sel = pick_rows(slot_refs[i][who : who + 1, :], capacity).astype(F32).astype(BF16)
            part = lax.dot_general(sel, rows[...], TN, preferred_element_type=F32)
            total = part if total is None else total + part
        outs[i][...] = total.astype(BF16)


def combine(rows, slots):
    blocks = len(slots)
    capacity, width = rows[0].shape
    tokens = slots[0].shape[1]
    vmem = pl.BlockSpec(memory_space=pltpu.VMEM)
    return pl.pallas_call(
        lambda *refs: combine_kernel(capacity, blocks, *refs),
        out_shape=[jax.ShapeDtypeStruct((tokens, width), BF16)] * blocks,
        in_specs=[vmem] * (3 * blocks),
        out_specs=[vmem] * blocks,
        compiler_params=pltpu.CompilerParams(vmem_limit_bytes=VMEM_LIMIT),
        cost_estimate=lasting(1.5 + 1.1 * blocks),
        name="combine_rows",
    )(*rows, *slots)


def wgrad_kernel(groups, gate_rows, down_rows, *refs):
    rows, ge, hid, dgu = (refs[i * groups : (i + 1) * groups] for i in range(4))
    out = refs[4 * groups]
    for left, right, start, count in (
        (rows, dgu, 0, gate_rows),
        (hid, ge, gate_rows, down_rows),
    ):
        total = None
        for g in range(groups):
            part = lax.dot_general(
                left[g][...], right[g][...], (((0,), (0,)), ((), ())), preferred_element_type=F32
            )
            total = part if total is None else total + part
        out[0, start : start + count, :] = total.astype(BF16)


def expert_wgrad(rows, ge, hid, dgu):
    devices = lax.axis_size("dp")
    groups = len(rows)
    width = rows[0].shape[1]
    hidden = hid[0].shape[1]
    gate_rows, down_rows = width // devices, hidden // devices
    if sum(array.shape[0] for array in rows) > 2048 or gate_rows % 128 or down_rows % 128:
        everything = [jnp.concatenate(part, axis=0) for part in (rows, ge, hid, dgu)]
        gate_up = jnp.dot(everything[0].T, everything[3], preferred_element_type=F32)
        down = jnp.dot(everything[2].T, everything[1], preferred_element_type=F32)
        return jnp.concatenate(
            [
                gate_up.astype(BF16).reshape(devices, gate_rows, 2 * hidden),
                down.astype(BF16).reshape(devices, down_rows, width),
            ],
            axis=1,
        )
    sliced = lambda size: [
        pl.BlockSpec((array.shape[0], size), lambda i: (0, i)) for array in rows
    ]
    fixed = lambda size: [
        pl.BlockSpec((array.shape[0], size), lambda i: (0, 0)) for array in rows
    ]
    return pl.pallas_call(
        lambda *refs: wgrad_kernel(groups, gate_rows, down_rows, *refs),
        grid=(devices,),
        out_shape=jax.ShapeDtypeStruct((devices, gate_rows + down_rows, width), BF16),
        in_specs=sliced(gate_rows) + fixed(width) + sliced(down_rows) + fixed(2 * hidden),
        out_specs=pl.BlockSpec((1, gate_rows + down_rows, width), lambda i: (i, 0, 0)),
        compiler_params=pltpu.CompilerParams(vmem_limit_bytes=VMEM_LIMIT),
        cost_estimate=lasting(12.5),
        name="expert_wgrad",
    )(*rows, *ge, *hid, *dgu)


def return_direct(partial):
    parity = lax.axis_index("expert") % 2
    return jnp.where(parity == 0, partial[2], partial[4])


def return_passed(partial):
    return mixed_hop(partial[6], 2, 4)


def return_onward(partial, passed):
    parity = lax.axis_index("expert") % 2
    rest = jnp.where(parity == 0, partial[4], partial[2]).astype(F32) + passed.astype(F32)
    return rest.astype(BF16)


def return_halving(partial):
    blocks = dict(partial)
    for bit in link_bits(lax.axis_size("expert")):
        arrived = {m: hop(blocks[m], "expert", bit) for m in blocks if m & bit}
        blocks = {
            m: (blocks[m].astype(F32) + arrived[m | bit].astype(F32)).astype(BF16)
            for m in blocks
            if not m & bit
        }
    return [blocks[0]]


def sum_terms(terms):
    total = terms[0].astype(F32)
    for term in terms[1:]:
        total = total + term.astype(F32)
    return total


def swap_halves(values):
    width = values.shape[1]
    half = HEAD_DIMENSION // 2
    lane = lax.broadcasted_iota(jnp.int32, values.shape, 1) % HEAD_DIMENSION
    return jnp.where(
        lane < half, pltpu.roll(values, width - half, 1), pltpu.roll(values, half, 1)
    )


def project_kernel(key_width, x_ref, gain_ref, w_ref, cos_ref, sin_ref, out_ref, xn_ref):
    step = pl.program_id(0)
    width = out_ref.shape[1]

    @pl.when(step == 0)
    def _():
        x = x_ref[...].astype(F32)
        inverse = lax.rsqrt(jnp.mean(x * x, axis=-1, keepdims=True) + eps_norm)
        xn_ref[...] = (x * inverse * gain_ref[...]).astype(BF16)

    before = jnp.dot(xn_ref[...], w_ref[...], preferred_element_type=F32)

    def turn(values):
        repeats = values.shape[1] // cos_ref.shape[1]
        cosine = jnp.concatenate([cos_ref[...]] * repeats, axis=1)
        sine = jnp.concatenate([sin_ref[...]] * repeats, axis=1)
        return values * cosine + swap_halves(values) * sine

    @pl.when(step == 0)
    def _():
        out_ref[...] = (turn(before) * HEAD_DIMENSION ** (-0.5)).astype(BF16)

    @pl.when(step == 1)
    def _():
        out_ref[:, :key_width] = turn(before[:, :key_width]).astype(BF16)
        out_ref[:, key_width:] = before[:, key_width:].astype(BF16)


def project(x, gain, weight, cosine, sine, query_width, key_width):
    rows, width = x.shape
    total = weight.shape[1]
    tile = query_width
    assert total == 2 * tile
    whole = lambda shape: pl.BlockSpec(shape, lambda i: (0, 0))
    return pl.pallas_call(
        lambda *refs: project_kernel(key_width, *refs),
        grid=(2,),
        out_shape=(
            jax.ShapeDtypeStruct((rows, total), BF16),
            jax.ShapeDtypeStruct((rows, width), BF16),
        ),
        in_specs=[
            whole((rows, width)),
            whole((1, width)),
            pl.BlockSpec((width, tile), lambda i: (0, i)),
            whole(cosine.shape),
            whole(sine.shape),
        ],
        out_specs=(pl.BlockSpec((rows, tile), lambda i: (0, i)), whole((rows, width))),
        compiler_params=pltpu.CompilerParams(vmem_limit_bytes=VMEM_LIMIT),
        cost_estimate=lasting(8.6),
        name="project_heads",
    )(x, gain, weight, cosine, sine)


def pair_of(block, which):
    values = block.astype(F32)
    low = lax.broadcasted_iota(jnp.int32, values.shape, 1) < HEAD_DIMENSION
    other = pltpu.roll(values, HEAD_DIMENSION, 1)
    return jnp.where(low, *((values, other) if which == 0 else (other, values))).astype(BF16)


def head_of(block, which):
    low = lax.broadcasted_iota(jnp.int32, block.shape, 1) < HEAD_DIMENSION
    return jnp.where(low if which == 0 else ~low, block.astype(F32), 0.0).astype(BF16)


def fill_bias(bias_ref, begin_ref):
    key = lax.broadcasted_iota(jnp.int32, bias_ref.shape, 0)
    query = lax.broadcasted_iota(jnp.int32, bias_ref.shape, 1)
    bias_ref[...] = jnp.where((key <= query) & (key >= begin_ref[...]), 0.0, -1e30)


def attend_kernel(tile, q_ref, k_ref, v_ref, begin_ref, out_ref, lse_ref, bias_ref):
    rows = q_ref.shape[0]
    lanes = 2 * HEAD_DIMENSION

    @pl.when(pl.program_id(0) == 0)
    def _():
        fill_bias(bias_ref, begin_ref)

    for c in range(2):
        place = slice(c * lanes, (c + 1) * lanes)
        keys = pair_of(k_ref[...], c)
        values = pair_of(v_ref[...], c)
        for start in range(0, rows, tile):
            span = slice(start, start + tile)
            reach = start + tile
            query = q_ref[span, place]
            outs = []
            for h in range(2):
                scores = lax.dot_general(
                    keys[:reach], head_of(query, h), NT, preferred_element_type=F32
                )
                scores = scores + bias_ref[:reach, span]
                peak = jnp.max(scores, axis=0, keepdims=True)
                raised = jnp.exp(scores - peak)
                total = jnp.sum(raised, axis=0, keepdims=True)
                mixed = lax.dot_general(
                    values[:reach], raised.astype(BF16), TN, preferred_element_type=F32
                )
                part = slice(h * HEAD_DIMENSION, (h + 1) * HEAD_DIMENSION)
                outs.append(mixed[part] * (1.0 / total))
                lse_ref[0, 2 * c + h : 2 * c + h + 1, span] = peak + jnp.log(total)
            out_ref[span, place] = jnp.concatenate(outs, axis=0).T.astype(BF16)


def attend(qkv, begin, query_width, key_width):
    rows = qkv.shape[0]
    lanes = 2 * HEAD_DIMENSION
    key_start = query_width // lanes
    value_start = (query_width + key_width) // lanes
    steps = key_width // lanes
    pair = pl.BlockSpec((rows, 2 * lanes), lambda i: (0, i))
    return pl.pallas_call(
        lambda *refs: attend_kernel(min(128, rows), *refs),
        grid=(steps,),
        out_shape=(
            jax.ShapeDtypeStruct((rows, query_width), BF16),
            jax.ShapeDtypeStruct((steps, 4, rows), F32),
        ),
        in_specs=[
            pair,
            pl.BlockSpec((rows, lanes), lambda i: (0, key_start + i)),
            pl.BlockSpec((rows, lanes), lambda i: (0, value_start + i)),
            pl.BlockSpec(begin.shape, lambda i: (0, 0)),
        ],
        out_specs=(pair, pl.BlockSpec((1, 4, rows), lambda i: (i, 0, 0))),
        scratch_shapes=[pltpu.VMEM((rows, rows), F32)],
        compiler_params=pltpu.CompilerParams(vmem_limit_bytes=VMEM_LIMIT),
        cost_estimate=lasting(11.5),
        name="attend",
    )(qkv, qkv, qkv, begin)


def attend_back_kernel(
    tile, q_ref, k_ref, v_ref, grad_ref, lse_ref, begin_ref, cos_ref, sin_ref,
    dq_ref, dk_ref, dv_ref, bias_ref, dk_sum, dv_sum,
):
    rows = q_ref.shape[0]
    lanes = 2 * HEAD_DIMENSION

    @pl.when(pl.program_id(0) == 0)
    def _():
        fill_bias(bias_ref, begin_ref)

    def turn_back(values, cosine, sine):
        return values * cosine - swap_halves(values) * sine

    for c in range(2):
        place = slice(c * lanes, (c + 1) * lanes)
        keys = pair_of(k_ref[...], c)
        values = pair_of(v_ref[...], c)
        for start in reversed(range(0, rows, tile)):
            span = slice(start, start + tile)
            reach = start + tile
            outs = []
            dk = dv = None
            for h in range(2):
                query = head_of(q_ref[span, place], h)
                grad = head_of(grad_ref[span, place], h)
                scores = lax.dot_general(keys[:reach], query, NT, preferred_element_type=F32)
                row = lse_ref[0, 2 * c + h : 2 * c + h + 1, span]
                probs = jnp.exp(scores + bias_ref[:reach, span] - row)
                grad_probs = lax.dot_general(values[:reach], grad, NT, preferred_element_type=F32)
                delta = jnp.sum(probs * grad_probs, axis=0, keepdims=True)
                grad_scores = (probs * (grad_probs - delta)).astype(BF16)
                turned = lax.dot_general(keys[:reach], grad_scores, TN, preferred_element_type=F32)
                outs.append(turned[h * HEAD_DIMENSION : (h + 1) * HEAD_DIMENSION])
                dk_part = jnp.dot(grad_scores, query, preferred_element_type=F32)
                dv_part = jnp.dot(probs.astype(BF16), grad, preferred_element_type=F32)
                dk = dk_part if dk is None else dk + dk_part
                dv = dv_part if dv is None else dv + dv_part
            if reach == rows:
                dk_sum[c] = dk
                dv_sum[c] = dv
            else:
                dk_sum[c, :reach, :] += dk
                dv_sum[c, :reach, :] += dv
            dq = turn_back(jnp.concatenate(outs, axis=0).T, cos_ref[span, :], sin_ref[span, :])
            dq_ref[span, place] = (dq * HEAD_DIMENSION ** (-0.5)).astype(BF16)
    low = lax.broadcasted_iota(jnp.int32, (rows, lanes), 1) < HEAD_DIMENSION

    def both(sums):
        return jnp.where(
            low, *(sums[c] + pltpu.roll(sums[c], HEAD_DIMENSION, 1) for c in range(2))
        )

    dk_ref[...] = turn_back(both(dk_sum), cos_ref[...], sin_ref[...]).astype(BF16)
    dv_ref[...] = both(dv_sum).astype(BF16)


def attend_back(qkv, grad, lse, begin, cosine, sine, query_width, key_width, first, count):
    rows = qkv.shape[0]
    lanes = 2 * HEAD_DIMENSION
    key_start = query_width // lanes + first
    value_start = (query_width + key_width) // lanes + first
    pair = pl.BlockSpec((rows, 2 * lanes), lambda i: (0, first + i))
    whole = lambda shape: pl.BlockSpec(shape, lambda i: (0, 0))
    return pl.pallas_call(
        lambda *refs: attend_back_kernel(min(256, rows), *refs),
        grid=(count,),
        out_shape=(
            jax.ShapeDtypeStruct((rows, 2 * lanes * count), BF16),
            jax.ShapeDtypeStruct((rows, lanes * count), BF16),
            jax.ShapeDtypeStruct((rows, lanes * count), BF16),
        ),
        in_specs=[
            pair,
            pl.BlockSpec((rows, lanes), lambda i: (0, key_start + i)),
            pl.BlockSpec((rows, lanes), lambda i: (0, value_start + i)),
            pair,
            pl.BlockSpec((1, 4, rows), lambda i: (first + i, 0, 0)),
            whole(begin.shape),
            whole(cosine.shape),
            whole(sine.shape),
        ],
        out_specs=(
            pl.BlockSpec((rows, 2 * lanes), lambda i: (0, i)),
            pl.BlockSpec((rows, lanes), lambda i: (0, i)),
            pl.BlockSpec((rows, lanes), lambda i: (0, i)),
        ),
        scratch_shapes=[
            pltpu.VMEM((rows, rows), F32),
            pltpu.VMEM((2, rows, lanes), F32),
            pltpu.VMEM((2, rows, lanes), F32),
        ],
        compiler_params=pltpu.CompilerParams(vmem_limit_bytes=VMEM_LIMIT),
        cost_estimate=lasting(5.1 * count),
        name="attend_back",
    )(qkv, qkv, qkv, grad, lse, begin, cosine, sine)


def attend_back_last(qkv, grad, lse, begin, cosine, sine, query_width, key_width, first, x, other):
    rows = qkv.shape[0]
    lanes = 2 * HEAD_DIMENSION
    height = x.shape[1]
    key_start = query_width // lanes + first
    value_start = (query_width + key_width) // lanes + first
    pair = pl.BlockSpec((rows, 2 * lanes), lambda i: (0, first))
    whole = lambda array: pl.BlockSpec(array.shape, lambda i: (0, 0))
    mine = [jax.ShapeDtypeStruct((rows, size), BF16) for size in (2 * lanes, lanes, lanes)]
    width = sum(array.shape[1] for array in (*other, *mine))
    halves = [jax.ShapeDtypeStruct((height // 2, width), BF16)] * 2
    shape = tuple((array.shape[1], 1) for array in (*other, *mine))

    def kernel(*refs):
        inputs, x_ref, others = refs[:8], refs[8], refs[9:12]
        outs, split, scratch = refs[12:15], refs[15:17], refs[17:]
        attend_back_kernel(min(256, rows), *inputs, *outs, *scratch)
        pairs = [ref for part in (*others, *outs) for ref in (x_ref, part)]
        split_kernel(shape, *pairs, *split)

    *part, keep, send = pl.pallas_call(
        kernel,
        grid=(1,),
        out_shape=(*mine, *halves),
        in_specs=[
            pair,
            pl.BlockSpec((rows, lanes), lambda i: (0, key_start)),
            pl.BlockSpec((rows, lanes), lambda i: (0, value_start)),
            pair,
            pl.BlockSpec((1, 4, rows), lambda i: (first, 0, 0)),
            *[whole(array) for array in (begin, cosine, sine, x, *other)],
        ],
        out_specs=[whole(array) for array in (*mine, *halves)],
        scratch_shapes=[
            pltpu.VMEM((rows, rows), F32),
            pltpu.VMEM((2, rows, lanes), F32),
            pltpu.VMEM((2, rows, lanes), F32),
        ],
        compiler_params=pltpu.CompilerParams(vmem_limit_bytes=VMEM_LIMIT),
        cost_estimate=lasting(10.0),
        name="attend_back_last",
    )(qkv, qkv, qkv, grad, lse, begin, cosine, sine, x, *other)
    return part, keep, send


def finish_kernel(parts, *refs):
    across_ref, other_ref, gain_ref = refs[:3]
    weights, outs = refs[3:6], refs[6:10]
    router_out, gain_one_out, gain_two_out, rows_ref, small_ref = refs[10:]
    chip, core = lax.axis_index("expert") // 2, lax.axis_index("expert") % 2
    rows = across_ref.shape[1]
    for m in range(across_ref.shape[0]):
        for ref, own in ((across_ref, core), (other_ref, 1 - core)):
            at = pl.multiple_of((chip ^ m) * 2 * rows + own * rows, rows)
            rows_ref[pl.ds(at, rows), :] = ref[m]
    start = 0
    filled = [0] * 5
    for which, width in parts:
        out, at = (*outs, small_ref)[which], filled[which]
        out[:, at : at + width] = rows_ref[:, start : start + width].astype(F32)
        filled[which] += width
        start += width
    total = None
    for weight, grad in zip(weights, outs):
        part = jnp.sum(weight[...].astype(F32) * grad[...], axis=-1, keepdims=True)
        total = part if total is None else total + part
    height = rows_ref.shape[0]
    same = lax.broadcasted_iota(jnp.int32, (height, height), 0) == lax.broadcasted_iota(
        jnp.int32, (height, height), 1
    )
    experts = router_out.shape[1]
    router_out[...] = small_ref[:, :experts]
    row = jnp.sum(jnp.where(same, total, 0.0), axis=0, keepdims=True)
    gain_one_out[...] = row / gain_ref[...].astype(F32)
    gain_two_out[...] = jnp.sum(
        jnp.where(same, small_ref[:, experts : experts + 1], 0.0), axis=0, keepdims=True
    )


def finish_grads(across, other, parts, experts, weights, gain):
    rows = across.shape[0] * 2 * across.shape[1]
    widths = [sum(w for which, w in parts if which == i) for i in range(5)]
    vmem = pl.BlockSpec(memory_space=pltpu.VMEM)
    shapes = [(rows, width) for width in (*widths[:4], experts)] + [(1, rows)] * 2
    return pl.pallas_call(
        lambda *refs: finish_kernel(parts, *refs),
        out_shape=[jax.ShapeDtypeStruct(shape, F32) for shape in shapes],
        in_specs=[vmem] * 6,
        out_specs=[vmem] * 7,
        scratch_shapes=[
            pltpu.VMEM((rows, across.shape[2]), BF16),
            pltpu.VMEM((rows, widths[4]), F32),
        ],
        compiler_params=pltpu.CompilerParams(vmem_limit_bytes=VMEM_LIMIT),
        cost_estimate=lasting(4.0),
        name="finish_grads",
    )(across, other, gain, *weights)


def local(
    tokens,
    lengths,
    routes,
    cotangent,
    gain_attn,
    w_query,
    key_projection_weight,
    value_projection_weight,
    w_out,
    gain_moe,
    w_router,
    w_gate,
    w_up,
    w_down,
):
    count_of_rows, model_width = tokens.shape
    expert_count = lax.axis_size("expert")
    devices = lax.axis_size("dp")
    e_index = lax.axis_index("expert")
    top_count = routes.shape[1]
    capacity = 2 * count_of_rows * top_count // expert_count
    shard_rows = gain_attn.shape[0]
    query_width = w_query.shape[1]
    key_width = key_projection_weight.shape[1]

    lanes = -(-(expert_count + 2) // 128) * 128
    small = jnp.concatenate(
        [
            w_router,
            gain_attn[:, None],
            gain_moe[:, None],
            jnp.zeros((shard_rows, lanes - expert_count - 2), BF16),
        ],
        axis=1,
    )
    routes_rel = gather_small(routes.T)
    (qkv_w, out_w, small_w), cot_blocks, _ = gather_weights(
        [w_query, key_projection_weight, value_projection_weight, w_out, small],
        (query_width + 2 * key_width, model_width, lanes),
        cotangent,
    )
    router_w = small_w[:, :expert_count]
    gains = small_w[:, expert_count : expert_count + 2].astype(F32).T
    gain_first, gain_second = gains[0], gains[1]

    index_rows = jnp.arange(count_of_rows, dtype=jnp.int32)
    before = (index_rows[:, None] < index_rows[None, :]).astype(BF16)

    def slots_of(expert):
        hit = jnp.any(routes_rel == expert, axis=1)
        place = jnp.dot(hit.astype(BF16), before, preferred_element_type=F32)
        return jnp.where(hit, place.astype(jnp.int32), -1)

    slots_mine = slots_of(e_index)
    slots_sibling = slots_of(e_index ^ 1)
    mine_row = (jnp.arange(lanes) == e_index).astype(F32)[None]
    gate_up_w = jnp.concatenate([w_gate[0], w_up[0]], axis=1)
    down_w = w_down[0]

    _, position = positions_of(lengths[0], count_of_rows)
    begin = (index_rows - position)[None]
    half = HEAD_DIMENSION // 2
    cosine, sine = rope_tables(position, HEAD_DIMENSION)
    cosine = jnp.concatenate([cosine] * 4, axis=1)
    sine = jnp.concatenate([-sine, sine] * 2, axis=1)

    qkv, first_normalized = project(
        tokens, gain_first[None], qkv_w, cosine, sine, query_width, key_width
    )
    attn_rows, lse = attend(qkv, begin, query_width, key_width)
    resid_in = tokens.astype(F32)
    resid_mid = resid_in + jnp.dot(attn_rows, out_w, preferred_element_type=F32)
    inverse_two = lax.rsqrt(jnp.mean(resid_mid * resid_mid, axis=-1, keepdims=True) + eps_norm)
    normed_two = (resid_mid * inverse_two * gain_second).astype(BF16)

    cot_list = [cot_blocks[m] for m in range(expert_count)]
    tok_blocks = {}

    logits = jnp.dot(normed_two, router_w, preferred_element_type=F32)
    expert_ids = jnp.arange(expert_count, dtype=jnp.int32)
    chosen = (routes[:, :, None] == expert_ids[None, None, :]).astype(F32)
    picked = jnp.sum(logits[:, None, :] * chosen, axis=-1)
    gates = jax.nn.softmax(picked, axis=-1)

    even = list(range(0, expert_count, 2))
    groups = [[0], [2, 4], [6]] if expert_count == 8 else [[m] for m in even]
    last_mask = even[-1]
    moe_rows_of, in_rows_of, saved, in_partial = {}, {}, [], {}
    slots_of_pair = {m: jnp.stack([slots_mine[m], slots_sibling[m]]) for m in even}

    def run_group(group):
        masks = [m for low_mask in group for m in (low_mask, low_mask ^ 1)]
        start = masks[0]
        results = expert_group(
            [tok_blocks[m] for m in masks],
            [cot_blocks[m] for m in masks],
            slots_mine[start : start + len(masks)],
            routes_rel[start : start + len(masks)],
            mine_row,
            small_w,
            gate_up_w,
            down_w,
            capacity,
        )
        for i, m in enumerate(masks):
            moe_rows_of[m] = results[i]
            in_rows_of[m] = results[len(masks) + i]
        saved.append(list(results[2 * len(masks) :]))

    def return_rows(group, *earlier):
        rows = []
        for m in group:
            arrived = hop(in_rows_of[m ^ 1], "expert", 1)
            keep = in_rows_of[m]
            rows += [after(keep, *earlier) if earlier else keep, arrived]
        in_partial.update(zip(group, combine(rows, [slots_of_pair[m] for m in group])))

    sent = after(normed_two, slots_mine, slots_sibling, *cot_list)
    tok_blocks[0] = sent
    tok_blocks[1] = hop(sent, "expert", 1)
    run_group([0])
    tok_blocks.update(gather_links(sent, lambda pair: after_all(pair, in_rows_of[0])))
    for m in even[1:]:
        tok_blocks[m ^ 1] = hop(tok_blocks[m], "expert", 1)
    direct = None
    for group in groups[1:]:
        if expert_count == 8:
            earlier = [in_rows_of[1]]
            if group == [last_mask]:
                return_rows([2, 4])
                direct_rows = return_direct(in_partial)
                direct = mixed_hop(direct_rows, 2, 4)
                earlier.append(direct_rows)
            tok_blocks[group[0]] = after(tok_blocks[group[0]], *earlier)
        run_group(group)
    if direct is None:
        for low_mask in even:
            return_rows([low_mask])
    else:
        return_rows([last_mask], direct)
        return_rows([0], in_partial[last_mask])
    saved[0][0] = after(saved[0][0], in_partial[last_mask])
    expert_grads = expert_wgrad(*[list(part) for part in zip(*saved)])
    if direct is None:
        grad_terms = return_halving(in_partial)
        passed = grad_terms[0]
    else:
        passed = after(return_passed(in_partial), expert_grads)
        onward = return_onward(in_partial, passed)
        grad_terms = [in_partial[0], direct, mixed_hop(onward, 4, 2)]
    expert_pieces = lax.psum_scatter(
        after(expert_grads, passed).reshape(-1, model_width), "dp", scatter_dimension=0, tiled=True
    )

    moe_rows = []
    for m in even:
        moe_rows += [moe_rows_of[m], hop(after(moe_rows_of[m ^ 1], passed), "expert", 1)]
    moe_slots = [slots_of_pair[m] for m in even]
    if expert_count == 8:
        moe_list = combine(moe_rows, moe_slots)
        grad_terms = after_all(grad_terms, *moe_list)
    else:
        moe_list = [
            combine(moe_rows[2 * i : 2 * i + 2], moe_slots[i : i + 1])[0]
            for i in range(len(moe_slots))
        ]
    moe_partial = dict(zip(even, moe_list))

    grad_final = cotangent.astype(F32)
    returned = sum_terms(grad_terms)
    gate_columns = returned[:, model_width : model_width + expert_count]
    gate_columns += returned[:, model_width + lanes // 2 :][:, :expert_count]
    grad_gates = jnp.sum(gate_columns[:, None, :] * chosen, axis=-1)
    grad_picked = gates * (grad_gates - jnp.sum(gates * grad_gates, axis=-1, keepdims=True))
    grad_logits = jnp.sum(grad_picked[:, :, None] * chosen, axis=1).astype(BF16)
    grad_normed_two = jnp.dot(grad_logits, router_w.T, preferred_element_type=F32)
    grad_normed_two = grad_normed_two + returned[:, :model_width]
    scaled_two = grad_normed_two * gain_second
    gain_terms = (grad_normed_two * resid_mid * inverse_two).astype(BF16)
    grad_mid = (
        grad_final
        + inverse_two * scaled_two
        - resid_mid
        * inverse_two
        * inverse_two
        * inverse_two
        * jnp.mean(resid_mid * scaled_two, axis=-1, keepdims=True)
    )
    grad_mid_low = grad_mid.astype(BF16)
    grad_attn = lax.dot_general(grad_mid_low, out_w, NT, preferred_element_type=F32).astype(BF16)

    pairs = key_width // (2 * HEAD_DIMENSION)
    cut = pairs // 2
    def back(grad, first, count):
        return attend_back(
            qkv, grad, lse, begin, cosine, sine, query_width, key_width, first, count
        )

    parts = [back(grad_attn, 0, cut)]
    if direct is None:
        moe_terms = return_halving(moe_partial)
        moe_first, moe_last = moe_terms, moe_terms[0]
    else:
        for m in (2, 4, 6):
            moe_partial[m] = after(moe_partial[m], grad_terms[-1])
        moe_first = return_onward(
            moe_partial, after(return_passed(moe_partial), parts[0][0])
        )
        direct_rows = after(return_direct(moe_partial), parts[0][0])
        moe_last = mixed_hop(moe_first, 4, 2)
        moe_terms = [
            moe_partial[0],
            mixed_hop(after(direct_rows, moe_last), 2, 4),
            moe_last,
        ]
        moe_first = (moe_first, direct_rows)
    logits_wide = jnp.pad(grad_logits, ((0, 0), (0, lanes - expert_count)))
    gain_column = jnp.broadcast_to(jnp.arange(lanes) == expert_count, logits_wide.shape)
    early_columns = [[(first_normalized, after(part, *moe_first))] for part in parts[0]]
    early_columns += [
        [(attn_rows, grad_mid_low)],
        [(normed_two, logits_wide), (gain_terms, gain_column.astype(BF16))],
    ]
    fast = model_width % (16 * devices * expert_count) == 0 and pairs == cut + 2
    if fast:
        early_keep, early_send = split_grads(early_columns)
        parts.append(back(after(grad_attn, early_send, moe_last), cut, 1))
        early_near = across_cores(
            early_keep,
            after(early_send, moe_last),
            lambda values: after(values, parts[1][0]),
        )
        part, late_keep, late_send = attend_back_last(
            qkv,
            after(grad_attn, early_near, moe_terms[1]),
            lse,
            begin,
            cosine,
            sine,
            query_width,
            key_width,
            cut + 1,
            first_normalized,
            parts[1],
        )
        parts.append(part)
        line_start, line_far = across_links_start(
            early_near, lambda pieces: after_all(pieces, late_send, expert_pieces)
        )
        late_arrival = hop(after(late_send, line_start), "expert", 1)
    else:
        parts.append(back(grad_attn, cut, pairs - cut))
        line_start = late_send = parts[1][0]
    resid_late, *moe_terms = after_all([resid_mid, *moe_terms], late_send)
    mixed_out = (resid_late + sum_terms(moe_terms)).astype(BF16)
    grad_qkv = jnp.concatenate(
        [after(part[i], line_start) for i in range(3) for part in parts], axis=1
    )
    grad_normed_one = lax.dot_general(grad_qkv, qkv_w, NT, preferred_element_type=F32)
    inverse_one = lax.rsqrt(jnp.mean(resid_in * resid_in, axis=-1, keepdims=True) + eps_norm)
    scaled_one = grad_normed_one * gain_first
    grad_input = (
        grad_mid
        + inverse_one * scaled_one
        - resid_in
        * inverse_one
        * inverse_one
        * inverse_one
        * jnp.mean(resid_in * scaled_one, axis=-1, keepdims=True)
    )
    gate_rows = model_width // devices
    hidden = down_w.shape[0]
    grad_input = grad_input.astype(BF16)
    expert_outs = [
        expert_pieces[None, :gate_rows, :hidden].astype(F32),
        expert_pieces[None, :gate_rows, hidden:].astype(F32),
        expert_pieces[None, gate_rows:, :].astype(F32),
    ]
    projections = (w_query, key_projection_weight, value_projection_weight)
    if fast:
        line_far, late_arrival = after_all([line_far, late_arrival], grad_input)
        late_near = join_cores(late_keep, late_arrival)
        late_line = across_links(late_near)
        early_line = (line_start + line_far.astype(F32)).astype(BF16)
        done = across_dp(
            jnp.concatenate([early_line, late_line], axis=-1),
            lambda pieces: after_all(pieces, mixed_out, *expert_outs),
        )
        across = jnp.stack([done] + [hop(done, "expert", m) for m in range(2, expert_count, 2)])
        names = [0, 1, 2, 3, 4] + [0, 1, 2] * 2
        sizes = [part.shape[1] for part in parts[0]] + [model_width, lanes]
        sizes += [part.shape[1] for later in parts[1:] for part in later]
        *columns, grad_out_part, grad_router_part, grad_gain_one, grad_gain_two = finish_grads(
            across,
            hop(across, "expert", 1),
            tuple(zip(names, sizes)),
            expert_count,
            projections,
            gain_attn[None],
        )
        grad_gain_one, grad_gain_two = grad_gain_one[0], grad_gain_two[0]
    else:
        products = [
            sum(lax.dot_general(a, d, TN, preferred_element_type=F32) for a, d in terms)
            for terms in early_columns + [[(first_normalized, part)] for part in parts[1]]
        ]
        total = jnp.concatenate(products, axis=1).astype(BF16)
        total = lax.psum_scatter(total, "dp", scatter_dimension=0, tiled=True)
        total = lax.psum(total, "expert").astype(F32)
        starts = [0]
        for product in products:
            starts.append(starts[-1] + product.shape[1])
        pieces = [total[:, a:d] for a, d in zip(starts, starts[1:])]
        columns = [jnp.concatenate([pieces[i], pieces[5 + i]], axis=1) for i in range(3)]
        grad_out_part, small_part = pieces[3:5]
        grad_router_part, grad_gain_two = small_part[:, :expert_count], small_part[:, expert_count]
        grad_gain_one = sum(
            jnp.sum(weight.astype(F32) * grad, axis=1)
            for weight, grad in zip(projections, columns)
        ) / gain_attn.astype(F32)
    return (
        mixed_out,
        grad_input,
        grad_gain_one,
        *columns,
        grad_out_part,
        grad_gain_two,
        grad_router_part,
        *expert_outs,
    )


def solution(mesh):
    placed = (
        P(("dp", "expert"), None),
        P(("dp", "expert"), None),
        P(("dp", "expert"), None),
        P(("dp", "expert"), None),
        P("dp"),
        P("dp", None),
        P("dp", None),
        P("dp", None),
        P("dp", None),
        P("dp"),
        P("dp", None),
        P("expert", None, None),
        P("expert", None, None),
        P("expert", None, None),
    )
    return jax.shard_map(
        local,
        mesh=mesh,
        in_specs=placed,
        out_specs=(
            P(("dp", "expert"), None),
            P(("dp", "expert"), None),
            P("dp"),
            P("dp", None),
            P("dp", None),
            P("dp", None),
            P("dp", None),
            P("dp"),
            P("dp", None),
            P("expert", "dp", None),
            P("expert", "dp", None),
            P("expert", "dp", None),
        ),
        check_vma=False,
    )
```

```python
import math

import jax
import jax.numpy as jnp
from jax import lax
from jax.experimental import pallas as pl
from jax.experimental.pallas import tpu as pltpu
from jax.sharding import PartitionSpec as P

QUERY_HEADS = 16
KEY_VALUE_HEADS = 8
HEAD_DIMENSION = 64


eps_norm = 1e-06


def positions_of(lengths_row, count_of_rows):
    index_rows = jnp.arange(count_of_rows, dtype=jnp.int32)
    ends = jnp.cumsum(lengths_row)
    member = jnp.sum((index_rows[:, None] >= ends[None, :]).astype(jnp.int32), axis=1)
    starts = ends - lengths_row
    onehot = member[:, None] == jnp.arange(lengths_row.shape[0], dtype=jnp.int32)[None, :]
    begin = jnp.sum(jnp.where(onehot, starts[None, :], 0), axis=1)
    return (member, index_rows - begin)


def rope_tables(positions, head_size):
    half_size = head_size // 2
    freq = jnp.exp(
        jnp.arange(half_size, dtype=jnp.float32) * (-2.0 * math.log(10000.0) / head_size)
    )
    angle = positions.astype(jnp.float32)[:, None] * freq[None, :]
    return (jnp.cos(angle), jnp.sin(angle))


F32 = jnp.float32
BF16 = jnp.bfloat16
VMEM_LIMIT = 56 * 1024 * 1024
NT = (((1,), (1,)), ((), ()))
TN = (((0,), (0,)), ((), ()))


def lasting(microseconds):
    return pl.CostEstimate(
        flops=int(microseconds * 1.15e9), bytes_accessed=1 << 20, transcendentals=0
    )


def hop(values, axis, mask):
    count = lax.axis_size(axis)
    return lax.ppermute(values, axis, [(i, i ^ mask) for i in range(count)])


def after_all(values, *earlier):
    return list(lax.optimization_barrier((*values, *earlier))[: len(values)])


def link_bits(count):
    return [1 << i for i in range(1, count.bit_length() - 1)]


def after(values, *earlier):
    return lax.optimization_barrier((values, *earlier))[0]


def mixed_hop(values, first, second):
    count = lax.axis_size("expert")
    return lax.ppermute(
        values, "expert", [(i, i ^ (second if i % 2 else first)) for i in range(count)]
    )


def gather_links(block, hold=lambda pair: pair):
    count = lax.axis_size("expert")
    blocks = {0: block}
    if count == 8:
        blocks[2], blocks[4] = hold((hop(block, "expert", 2), hop(block, "expert", 4)))
        parity = lax.axis_index("expert") % 2
        blocks[6] = mixed_hop(jnp.where(parity == 0, blocks[2], blocks[4]), 4, 2)
        return blocks
    for bit in link_bits(count):
        for m in list(blocks):
            blocks[m ^ bit] = hop(blocks[m], "expert", bit)
    return blocks


def gather_plane(block):
    blocks = gather_links(block)
    for m in list(blocks):
        blocks[m ^ 1] = hop(blocks[m], "expert", 1)
    return blocks


def gather_small(values):
    count = lax.axis_size("expert")
    rows = values[None]
    bit = 1
    while bit < count:
        rows = jnp.concatenate([rows, hop(rows, "expert", bit)], axis=0)
        bit *= 2
    return rows


def place_kernel(devices, rows, *refs):
    near, own_ref, outs = refs[:-4], refs[-4], refs[-3:]
    z_index = lax.axis_index("dp")
    e_index = lax.axis_index("expert")
    shard_rows = own_ref.shape[0]

    def put(at, count, values):
        column = 0
        for out in outs:
            width = out.shape[1]
            out[pl.ds(pl.multiple_of(at, 16), count), :] = values[:, column : column + width]
            column += width

    put(z_index * shard_rows, shard_rows, own_ref[...])
    for m, block in enumerate(near):
        for zm in range(1, devices):
            at = (z_index ^ zm) * shard_rows + (e_index ^ m) * rows
            put(at, rows, block[(zm - 1) * rows : zm * rows, :])


def gather_weights(shards, widths, cotangent):
    devices = lax.axis_size("dp")
    count = lax.axis_size("expert")
    shard_rows = shards[0].shape[0]
    rows = shard_rows // count
    if rows % 16 or count != 8:
        whole = lax.all_gather(jnp.concatenate(shards, axis=1), "dp", axis=0, tiled=True)
        starts = [sum(widths[:i]) for i in range(len(widths))]
        arrays = [whole[:, s : s + w] for s, w in zip(starts, widths)]
        return arrays, gather_plane(cotangent), whole
    start = lax.axis_index("expert") * rows
    mine = jnp.concatenate(
        [lax.dynamic_slice_in_dim(shard, start, rows, 0) for shard in shards], axis=1
    )
    far = jnp.concatenate([hop(mine, "dp", m) for m in range(1, devices)], axis=0)
    cotangent = after(cotangent, mine)
    cot = {0: cotangent, 2: hop(cotangent, "expert", 2), 4: hop(cotangent, "expert", 4)}
    far = after(far, cot[2], cot[4])
    near = gather_links(far)
    for m in (0, 2, 4):
        near[m ^ 1] = hop(near[m], "expert", 1)
    near[7] = hop(after(near[6], near[1], near[3], near[5]), "expert", 1)
    parity = lax.axis_index("expert") % 2
    cot[6] = mixed_hop(after(jnp.where(parity == 0, cot[2], cot[4]), near[6]), 4, 2)
    for m in list(cot):
        cot[m ^ 1] = hop(after(cot[m], near[7]), "expert", 1)
    vmem = pl.BlockSpec(memory_space=pltpu.VMEM)
    arrays = pl.pallas_call(
        lambda *refs: place_kernel(devices, rows, *refs),
        out_shape=[
            jax.ShapeDtypeStruct((shard_rows * devices, width), mine.dtype) for width in widths
        ],
        in_specs=[vmem] * (count + 1),
        out_specs=[vmem] * len(widths),
        compiler_params=pltpu.CompilerParams(vmem_limit_bytes=VMEM_LIMIT),
        cost_estimate=lasting(6.0),
        name="place_weights",
    )(*[near[m] for m in range(count)], jnp.concatenate(shards, axis=1))
    return arrays, cot, near[7]


def split_kernel(columns, *refs):
    keep_ref, send_ref = refs[-2:]
    core = lax.axis_index("expert") % 2
    rows = keep_ref.shape[0] * 2
    group = rows // (lax.axis_size("dp") * lax.axis_size("expert"))
    start = at = 0
    for width, terms in columns:
        total = None
        for _ in range(terms):
            part = lax.dot_general(
                refs[at][...], refs[at + 1][...], TN, preferred_element_type=F32
            )
            total = part if total is None else total + part
            at += 2
        low = total.astype(BF16)
        place = slice(start, start + width)
        start += width
        for who, (even, odd) in enumerate(((keep_ref, send_ref), (send_ref, keep_ref))):

            @pl.when(core == who)
            def _(even=even, odd=odd, low=low, place=place):
                for i in range(rows // group):
                    out = odd if i % 2 else even
                    out[i // 2 * group : (i // 2 + 1) * group, place] = low[
                        i * group : (i + 1) * group, :
                    ]


def split_grads(columns):
    height = columns[0][0][0].shape[1]
    widths = [terms[0][1].shape[1] for terms in columns]
    width = sum(widths)
    vmem = pl.BlockSpec(memory_space=pltpu.VMEM)
    operands = [array for terms in columns for pair in terms for array in pair]
    shape = tuple((w, len(terms)) for w, terms in zip(widths, columns))
    return pl.pallas_call(
        lambda *refs: split_kernel(shape, *refs),
        out_shape=(jax.ShapeDtypeStruct((height // 2, width), BF16),) * 2,
        in_specs=[vmem] * len(operands),
        out_specs=(vmem, vmem),
        compiler_params=pltpu.CompilerParams(vmem_limit_bytes=VMEM_LIMIT),
        cost_estimate=lasting(1.0 + 5.0 * width / height),
        name="weight_grads",
    )(*operands)


def pick(values, index, axis):
    return lax.dynamic_index_in_dim(values, index, axis, keepdims=False)


def join_cores(keep, arrived, hold=lambda values: values):
    near = hold(keep.astype(F32) + arrived.astype(F32)).astype(BF16)
    devices, chips = lax.axis_size("dp"), lax.axis_size("expert") // 2
    return near.reshape(devices, chips, -1, near.shape[-1])


def across_cores(keep, send, hold=lambda values: values):
    return join_cores(keep, hop(send, "expert", 1), hold)


def across_links(near, hold=lambda pieces: pieces):
    chip = lax.axis_index("expert") // 2
    pieces = [
        hop(pick(near, chip ^ m, 1), "expert", 2 * m).astype(F32) for m in range(1, near.shape[1])
    ]
    line = pick(near, chip, 1).astype(F32)
    for piece in hold(pieces):
        line = line + piece
    return line.astype(BF16)


def across_links_start(near, hold):
    chip, across = lax.axis_index("expert") // 2, near.shape[1] - 1
    pieces = [
        hop(pick(near, chip ^ m, 1), "expert", 2 * m) for m in range(1, across + 1)
    ]
    line = pick(near, chip, 1).astype(F32)
    for piece in hold(pieces[:1]):
        line = line + piece.astype(F32)
    return line, pieces[1:]


def across_dp(line, hold=lambda pieces: pieces):
    z_index = lax.axis_index("dp")
    pieces = [hop(pick(line, z_index ^ m, 0), "dp", m) for m in range(1, line.shape[0])]
    done = pick(line, z_index, 0).astype(F32)
    for piece in hold(pieces):
        done = done + piece.astype(F32)
    return done.astype(BF16)


def pick_rows(slots, capacity):
    index = lax.broadcasted_iota(jnp.int32, (capacity, slots.shape[1]), 0)
    return index == slots


def expert_kernel(capacity, blocks, *refs):
    tok_hbm, cot_hbm = refs[:blocks], refs[blocks : 2 * blocks]
    slot_ref, route_ref, mine_ref, *weights_hbm = refs[2 * blocks : 2 * blocks + 6]
    refs = refs[2 * blocks + 6 :]
    count = 2 * blocks + 4
    outs, refs = refs[:count], refs[count:]
    tok, cot, refs = refs[:blocks], refs[blocks : 2 * blocks], refs[2 * blocks :]
    weights, stores = refs[:3], refs[3 : 3 + count]
    chosen_ref, sems = refs[3 + count :]
    router_ref, gate_up_ref, down_ref = weights
    rows_ref, ge_ref, hid_ref, dgu_ref = stores[2 * blocks :]
    pairs = [pair for i in range(blocks) for pair in ((tok_hbm[i], tok[i]), (cot_hbm[i], cot[i]))]
    pairs[2:2] = list(zip(weights_hbm, weights))
    loads = [
        pltpu.make_async_copy(source, target, sems.at[i])
        for i, (source, target) in enumerate(pairs)
    ]
    for load in loads:
        load.start()
    writes = []

    def write(index, place=None):
        source, target = stores[index], outs[index]
        if place is not None:
            source, target = source.at[place, :], target.at[place, :]
        copy = pltpu.make_async_copy(source, target, sems.at[len(loads) + len(writes)])
        copy.start()
        writes.append(copy)

    tokens = tok[0].shape[0]
    lanes = mine_ref.shape[1]
    top = route_ref.shape[1]
    hidden_width = hid_ref.shape[1]
    for b in range(blocks):
        place = pl.ds(b * capacity, capacity)
        loads[3 + 2 * b if b else 0].wait()
        picked = pick_rows(slot_ref[b : b + 1, :], capacity)
        sel = picked.astype(F32).astype(BF16)
        rows = jnp.dot(sel, tok[b][...], preferred_element_type=F32).astype(BF16)
        rows_ref[place, :] = rows
        write(2 * blocks, place)
        loads[4 + 2 * b if b else 1].wait()
        drows = jnp.dot(sel, cot[b][...], preferred_element_type=F32)
        expert = lax.broadcasted_iota(jnp.int32, (lanes, tokens), 0)
        named = route_ref[b, 0:1, :] == expert
        for k in range(1, top):
            named = named | (route_ref[b, k : k + 1, :] == expert)
        chosen_ref[...] = lax.dot_general(
            sel, named.astype(F32).astype(BF16), NT, preferred_element_type=F32
        )
        if b == 0:
            loads[2].wait()
        logits = jnp.dot(rows, router_ref[...], preferred_element_type=F32)
        chosen = chosen_ref[...] > 0.5
        shown = jnp.where(chosen, logits, -1e30)
        weight = jnp.where(chosen, jnp.exp(shown - jnp.max(shown, axis=-1, keepdims=True)), 0.0)
        total = jnp.sum(weight, axis=-1, keepdims=True)
        gate = jnp.sum(weight * mine_ref[...], axis=-1, keepdims=True) / jnp.where(
            total > 0.0, total, 1.0
        )
        grad_out = (gate * drows).astype(BF16)
        ge_ref[place, :] = grad_out
        write(2 * blocks + 1, place)
        if b == 0:
            loads[3].wait()
        gate_up = jnp.dot(rows, gate_up_ref[...], preferred_element_type=F32)
        gate_pre = gate_up[:, :hidden_width]
        up_pre = gate_up[:, hidden_width:]
        if b == 0:
            loads[4].wait()
        grad_hidden = lax.dot_general(grad_out, down_ref[...], NT, preferred_element_type=F32)
        sigm = 1.0 / (1.0 + jnp.exp(-gate_pre))
        activated = gate_pre * sigm
        hidden = (activated * up_pre).astype(BF16)
        hid_ref[place, :] = hidden
        write(2 * blocks + 2, place)
        dgate = (grad_hidden * up_pre * sigm * (1.0 + gate_pre * (1.0 - sigm))).astype(BF16)
        dup = (grad_hidden * activated).astype(BF16)
        dgu_ref[place, :hidden_width] = dgate
        dgu_ref[place, hidden_width:] = dup
        write(2 * blocks + 3, place)
        back = stores[blocks + b]
        width = rows.shape[1]
        back[:, :width] = lax.dot_general(
            dgu_ref[place, :], gate_up_ref[...], NT, preferred_element_type=F32
        ).astype(BF16)
        result = jnp.dot(hidden, down_ref[...], preferred_element_type=F32)
        result = result.astype(BF16).astype(F32)
        moe = stores[b]
        moe[...] = (gate * result).astype(BF16)
        write(b)
        gate_grad = jnp.sum(drows * result, axis=-1, keepdims=True)
        high = gate_grad.astype(BF16).astype(F32)
        mine = mine_ref[...]
        back[:, width:] = (
            high * mine + (gate_grad - high) * pltpu.roll(mine, lanes // 2, 1)
        ).astype(BF16)
        write(blocks + b)
    for copy in writes:
        copy.wait()


def expert_group(tok, cot, slots, routes, mine, router, gate_up, down, capacity):
    blocks = len(tok)
    width = tok[0].shape[1]
    hidden = down.shape[0]
    tokens = slots.shape[1]
    rows = blocks * capacity
    vmem = pl.BlockSpec(memory_space=pltpu.VMEM)
    far = pl.BlockSpec(memory_space=pl.ANY)
    wide = width + mine.shape[1]
    shapes = [(capacity, width)] * blocks + [(capacity, wide)] * blocks
    shapes += [(rows, width), (rows, width), (rows, hidden)]
    shapes.append((rows, 2 * hidden))
    return pl.pallas_call(
        lambda *refs: expert_kernel(capacity, blocks, *refs),
        out_shape=[jax.ShapeDtypeStruct(shape, BF16) for shape in shapes],
        in_specs=[far] * (2 * blocks) + [vmem] * 3 + [far] * 3,
        out_specs=[far] * len(shapes),
        scratch_shapes=[pltpu.VMEM((tokens, width), BF16)] * (2 * blocks)
        + [pltpu.VMEM(array.shape, BF16) for array in (router, gate_up, down)]
        + [pltpu.VMEM(shape, BF16) for shape in shapes]
        + [
            pltpu.VMEM((capacity, mine.shape[1]), F32),
            pltpu.SemaphoreType.DMA((2 * blocks + 3 + 6 * blocks,)),
        ],
        compiler_params=pltpu.CompilerParams(vmem_limit_bytes=VMEM_LIMIT),
        cost_estimate=lasting(2.5 + 4.0 * blocks),
        name="expert_group",
    )(*tok, *cot, slots, routes, mine, router, gate_up, down)


def combine_kernel(capacity, blocks, *refs):
    slot_refs = refs[2 * blocks : 3 * blocks]
    outs = refs[3 * blocks :]
    for i in range(blocks):
        total = None
        for who, rows in enumerate(refs[2 * i : 2 * i + 2]):
            sel = pick_rows(slot_refs[i][who : who + 1, :], capacity).astype(F32).astype(BF16)
            part = lax.dot_general(sel, rows[...], TN, preferred_element_type=F32)
            total = part if total is None else total + part
        outs[i][...] = total.astype(BF16)


def combine(rows, slots):
    blocks = len(slots)
    capacity, width = rows[0].shape
    tokens = slots[0].shape[1]
    vmem = pl.BlockSpec(memory_space=pltpu.VMEM)
    return pl.pallas_call(
        lambda *refs: combine_kernel(capacity, blocks, *refs),
        out_shape=[jax.ShapeDtypeStruct((tokens, width), BF16)] * blocks,
        in_specs=[vmem] * (3 * blocks),
        out_specs=[vmem] * blocks,
        compiler_params=pltpu.CompilerParams(vmem_limit_bytes=VMEM_LIMIT),
        cost_estimate=lasting(1.5 + 1.1 * blocks),
        name="combine_rows",
    )(*rows, *slots)


def wgrad_kernel(groups, gate_rows, down_rows, *refs):
    rows, ge, hid, dgu = (refs[i * groups : (i + 1) * groups] for i in range(4))
    out = refs[4 * groups]
    for left, right, start, count in (
        (rows, dgu, 0, gate_rows),
        (hid, ge, gate_rows, down_rows),
    ):
        total = None
        for g in range(groups):
            part = lax.dot_general(
                left[g][...], right[g][...], (((0,), (0,)), ((), ())), preferred_element_type=F32
            )
            total = part if total is None else total + part
        out[0, start : start + count, :] = total.astype(BF16)


def expert_wgrad(rows, ge, hid, dgu):
    devices = lax.axis_size("dp")
    groups = len(rows)
    width = rows[0].shape[1]
    hidden = hid[0].shape[1]
    gate_rows, down_rows = width // devices, hidden // devices
    if sum(array.shape[0] for array in rows) > 2048 or gate_rows % 128 or down_rows % 128:
        everything = [jnp.concatenate(part, axis=0) for part in (rows, ge, hid, dgu)]
        gate_up = jnp.dot(everything[0].T, everything[3], preferred_element_type=F32)
        down = jnp.dot(everything[2].T, everything[1], preferred_element_type=F32)
        return jnp.concatenate(
            [
                gate_up.astype(BF16).reshape(devices, gate_rows, 2 * hidden),
                down.astype(BF16).reshape(devices, down_rows, width),
            ],
            axis=1,
        )
    sliced = lambda size: [
        pl.BlockSpec((array.shape[0], size), lambda i: (0, i)) for array in rows
    ]
    fixed = lambda size: [
        pl.BlockSpec((array.shape[0], size), lambda i: (0, 0)) for array in rows
    ]
    return pl.pallas_call(
        lambda *refs: wgrad_kernel(groups, gate_rows, down_rows, *refs),
        grid=(devices,),
        out_shape=jax.ShapeDtypeStruct((devices, gate_rows + down_rows, width), BF16),
        in_specs=sliced(gate_rows) + fixed(width) + sliced(down_rows) + fixed(2 * hidden),
        out_specs=pl.BlockSpec((1, gate_rows + down_rows, width), lambda i: (i, 0, 0)),
        compiler_params=pltpu.CompilerParams(vmem_limit_bytes=VMEM_LIMIT),
        cost_estimate=lasting(12.5),
        name="expert_wgrad",
    )(*rows, *ge, *hid, *dgu)


def return_direct(partial):
    parity = lax.axis_index("expert") % 2
    return jnp.where(parity == 0, partial[2], partial[4])


def return_passed(partial):
    return mixed_hop(partial[6], 2, 4)


def return_onward(partial, passed):
    parity = lax.axis_index("expert") % 2
    rest = jnp.where(parity == 0, partial[4], partial[2]).astype(F32) + passed.astype(F32)
    return rest.astype(BF16)


def return_halving(partial):
    blocks = dict(partial)
    for bit in link_bits(lax.axis_size("expert")):
        arrived = {m: hop(blocks[m], "expert", bit) for m in blocks if m & bit}
        blocks = {
            m: (blocks[m].astype(F32) + arrived[m | bit].astype(F32)).astype(BF16)
            for m in blocks
            if not m & bit
        }
    return [blocks[0]]


def sum_terms(terms):
    total = terms[0].astype(F32)
    for term in terms[1:]:
        total = total + term.astype(F32)
    return total


def swap_halves(values):
    width = values.shape[1]
    half = HEAD_DIMENSION // 2
    lane = lax.broadcasted_iota(jnp.int32, values.shape, 1) % HEAD_DIMENSION
    return jnp.where(
        lane < half, pltpu.roll(values, width - half, 1), pltpu.roll(values, half, 1)
    )


def project_kernel(key_width, x_ref, gain_ref, w_ref, cos_ref, sin_ref, out_ref, xn_ref):
    step = pl.program_id(0)
    width = out_ref.shape[1]

    @pl.when(step == 0)
    def _():
        x = x_ref[...].astype(F32)
        inverse = lax.rsqrt(jnp.mean(x * x, axis=-1, keepdims=True) + eps_norm)
        xn_ref[...] = (x * inverse * gain_ref[...]).astype(BF16)

    before = jnp.dot(xn_ref[...], w_ref[...], preferred_element_type=F32)

    def turn(values):
        repeats = values.shape[1] // cos_ref.shape[1]
        cosine = jnp.concatenate([cos_ref[...]] * repeats, axis=1)
        sine = jnp.concatenate([sin_ref[...]] * repeats, axis=1)
        return values * cosine + swap_halves(values) * sine

    @pl.when(step == 0)
    def _():
        out_ref[...] = (turn(before) * HEAD_DIMENSION ** (-0.5)).astype(BF16)

    @pl.when(step == 1)
    def _():
        out_ref[:, :key_width] = turn(before[:, :key_width]).astype(BF16)
        out_ref[:, key_width:] = before[:, key_width:].astype(BF16)


def project(x, gain, weight, cosine, sine, query_width, key_width):
    rows, width = x.shape
    total = weight.shape[1]
    tile = query_width
    assert total == 2 * tile
    whole = lambda shape: pl.BlockSpec(shape, lambda i: (0, 0))
    return pl.pallas_call(
        lambda *refs: project_kernel(key_width, *refs),
        grid=(2,),
        out_shape=(
            jax.ShapeDtypeStruct((rows, total), BF16),
            jax.ShapeDtypeStruct((rows, width), BF16),
        ),
        in_specs=[
            whole((rows, width)),
            whole((1, width)),
            pl.BlockSpec((width, tile), lambda i: (0, i)),
            whole(cosine.shape),
            whole(sine.shape),
        ],
        out_specs=(pl.BlockSpec((rows, tile), lambda i: (0, i)), whole((rows, width))),
        compiler_params=pltpu.CompilerParams(vmem_limit_bytes=VMEM_LIMIT),
        cost_estimate=lasting(8.6),
        name="project_heads",
    )(x, gain, weight, cosine, sine)


def pair_of(block, which):
    values = block.astype(F32)
    low = lax.broadcasted_iota(jnp.int32, values.shape, 1) < HEAD_DIMENSION
    other = pltpu.roll(values, HEAD_DIMENSION, 1)
    return jnp.where(low, *((values, other) if which == 0 else (other, values))).astype(BF16)


def head_of(block, which):
    low = lax.broadcasted_iota(jnp.int32, block.shape, 1) < HEAD_DIMENSION
    return jnp.where(low if which == 0 else ~low, block.astype(F32), 0.0).astype(BF16)


def fill_bias(bias_ref, begin_ref):
    key = lax.broadcasted_iota(jnp.int32, bias_ref.shape, 0)
    query = lax.broadcasted_iota(jnp.int32, bias_ref.shape, 1)
    bias_ref[...] = jnp.where((key <= query) & (key >= begin_ref[...]), 0.0, -1e30)


def attend_kernel(tile, q_ref, k_ref, v_ref, begin_ref, out_ref, lse_ref, bias_ref):
    rows = q_ref.shape[0]
    lanes = 2 * HEAD_DIMENSION

    @pl.when(pl.program_id(0) == 0)
    def _():
        fill_bias(bias_ref, begin_ref)

    for c in range(2):
        place = slice(c * lanes, (c + 1) * lanes)
        keys = pair_of(k_ref[...], c)
        values = pair_of(v_ref[...], c)
        for start in range(0, rows, tile):
            span = slice(start, start + tile)
            reach = start + tile
            query = q_ref[span, place]
            outs = []
            for h in range(2):
                scores = lax.dot_general(
                    keys[:reach], head_of(query, h), NT, preferred_element_type=F32
                )
                scores = scores + bias_ref[:reach, span]
                peak = jnp.max(scores, axis=0, keepdims=True)
                raised = jnp.exp(scores - peak)
                total = jnp.sum(raised, axis=0, keepdims=True)
                mixed = lax.dot_general(
                    values[:reach], raised.astype(BF16), TN, preferred_element_type=F32
                )
                part = slice(h * HEAD_DIMENSION, (h + 1) * HEAD_DIMENSION)
                outs.append(mixed[part] * (1.0 / total))
                lse_ref[0, 2 * c + h : 2 * c + h + 1, span] = peak + jnp.log(total)
            out_ref[span, place] = jnp.concatenate(outs, axis=0).T.astype(BF16)


def attend(qkv, begin, query_width, key_width):
    rows = qkv.shape[0]
    lanes = 2 * HEAD_DIMENSION
    key_start = query_width // lanes
    value_start = (query_width + key_width) // lanes
    steps = key_width // lanes
    pair = pl.BlockSpec((rows, 2 * lanes), lambda i: (0, i))
    return pl.pallas_call(
        lambda *refs: attend_kernel(min(128, rows), *refs),
        grid=(steps,),
        out_shape=(
            jax.ShapeDtypeStruct((rows, query_width), BF16),
            jax.ShapeDtypeStruct((steps, 4, rows), F32),
        ),
        in_specs=[
            pair,
            pl.BlockSpec((rows, lanes), lambda i: (0, key_start + i)),
            pl.BlockSpec((rows, lanes), lambda i: (0, value_start + i)),
            pl.BlockSpec(begin.shape, lambda i: (0, 0)),
        ],
        out_specs=(pair, pl.BlockSpec((1, 4, rows), lambda i: (i, 0, 0))),
        scratch_shapes=[pltpu.VMEM((rows, rows), F32)],
        compiler_params=pltpu.CompilerParams(vmem_limit_bytes=VMEM_LIMIT),
        cost_estimate=lasting(11.5),
        name="attend",
    )(qkv, qkv, qkv, begin)


def attend_back_kernel(
    tile, q_ref, k_ref, v_ref, grad_ref, lse_ref, begin_ref, cos_ref, sin_ref,
    dq_ref, dk_ref, dv_ref, bias_ref, dk_sum, dv_sum,
):
    rows = q_ref.shape[0]
    lanes = 2 * HEAD_DIMENSION

    @pl.when(pl.program_id(0) == 0)
    def _():
        fill_bias(bias_ref, begin_ref)

    def turn_back(values, cosine, sine):
        return values * cosine - swap_halves(values) * sine

    for c in range(2):
        place = slice(c * lanes, (c + 1) * lanes)
        keys = pair_of(k_ref[...], c)
        values = pair_of(v_ref[...], c)
        for start in reversed(range(0, rows, tile)):
            span = slice(start, start + tile)
            reach = start + tile
            outs = []
            dk = dv = None
            for h in range(2):
                query = head_of(q_ref[span, place], h)
                grad = head_of(grad_ref[span, place], h)
                scores = lax.dot_general(keys[:reach], query, NT, preferred_element_type=F32)
                row = lse_ref[0, 2 * c + h : 2 * c + h + 1, span]
                probs = jnp.exp(scores + bias_ref[:reach, span] - row)
                grad_probs = lax.dot_general(values[:reach], grad, NT, preferred_element_type=F32)
                delta = jnp.sum(probs * grad_probs, axis=0, keepdims=True)
                grad_scores = (probs * (grad_probs - delta)).astype(BF16)
                turned = lax.dot_general(keys[:reach], grad_scores, TN, preferred_element_type=F32)
                outs.append(turned[h * HEAD_DIMENSION : (h + 1) * HEAD_DIMENSION])
                dk_part = jnp.dot(grad_scores, query, preferred_element_type=F32)
                dv_part = jnp.dot(probs.astype(BF16), grad, preferred_element_type=F32)
                dk = dk_part if dk is None else dk + dk_part
                dv = dv_part if dv is None else dv + dv_part
            if reach == rows:
                dk_sum[c] = dk
                dv_sum[c] = dv
            else:
                dk_sum[c, :reach, :] += dk
                dv_sum[c, :reach, :] += dv
            dq = turn_back(jnp.concatenate(outs, axis=0).T, cos_ref[span, :], sin_ref[span, :])
            dq_ref[span, place] = (dq * HEAD_DIMENSION ** (-0.5)).astype(BF16)
    low = lax.broadcasted_iota(jnp.int32, (rows, lanes), 1) < HEAD_DIMENSION

    def both(sums):
        return jnp.where(
            low, *(sums[c] + pltpu.roll(sums[c], HEAD_DIMENSION, 1) for c in range(2))
        )

    dk_ref[...] = turn_back(both(dk_sum), cos_ref[...], sin_ref[...]).astype(BF16)
    dv_ref[...] = both(dv_sum).astype(BF16)


def attend_back(qkv, grad, lse, begin, cosine, sine, query_width, key_width, first, count):
    rows = qkv.shape[0]
    lanes = 2 * HEAD_DIMENSION
    key_start = query_width // lanes + first
    value_start = (query_width + key_width) // lanes + first
    pair = pl.BlockSpec((rows, 2 * lanes), lambda i: (0, first + i))
    whole = lambda shape: pl.BlockSpec(shape, lambda i: (0, 0))
    return pl.pallas_call(
        lambda *refs: attend_back_kernel(min(256, rows), *refs),
        grid=(count,),
        out_shape=(
            jax.ShapeDtypeStruct((rows, 2 * lanes * count), BF16),
            jax.ShapeDtypeStruct((rows, lanes * count), BF16),
            jax.ShapeDtypeStruct((rows, lanes * count), BF16),
        ),
        in_specs=[
            pair,
            pl.BlockSpec((rows, lanes), lambda i: (0, key_start + i)),
            pl.BlockSpec((rows, lanes), lambda i: (0, value_start + i)),
            pair,
            pl.BlockSpec((1, 4, rows), lambda i: (first + i, 0, 0)),
            whole(begin.shape),
            whole(cosine.shape),
            whole(sine.shape),
        ],
        out_specs=(
            pl.BlockSpec((rows, 2 * lanes), lambda i: (0, i)),
            pl.BlockSpec((rows, lanes), lambda i: (0, i)),
            pl.BlockSpec((rows, lanes), lambda i: (0, i)),
        ),
        scratch_shapes=[
            pltpu.VMEM((rows, rows), F32),
            pltpu.VMEM((2, rows, lanes), F32),
            pltpu.VMEM((2, rows, lanes), F32),
        ],
        compiler_params=pltpu.CompilerParams(vmem_limit_bytes=VMEM_LIMIT),
        cost_estimate=lasting(5.1 * count),
        name="attend_back",
    )(qkv, qkv, qkv, grad, lse, begin, cosine, sine)


def attend_back_last(qkv, grad, lse, begin, cosine, sine, query_width, key_width, first, x, other):
    rows = qkv.shape[0]
    lanes = 2 * HEAD_DIMENSION
    height = x.shape[1]
    key_start = query_width // lanes + first
    value_start = (query_width + key_width) // lanes + first
    pair = pl.BlockSpec((rows, 2 * lanes), lambda i: (0, first))
    whole = lambda array: pl.BlockSpec(array.shape, lambda i: (0, 0))
    mine = [jax.ShapeDtypeStruct((rows, size), BF16) for size in (2 * lanes, lanes, lanes)]
    width = sum(array.shape[1] for array in (*other, *mine))
    halves = [jax.ShapeDtypeStruct((height // 2, width), BF16)] * 2
    shape = tuple((array.shape[1], 1) for array in (*other, *mine))

    def kernel(*refs):
        inputs, x_ref, others = refs[:8], refs[8], refs[9:12]
        outs, split, scratch = refs[12:15], refs[15:17], refs[17:]
        attend_back_kernel(min(256, rows), *inputs, *outs, *scratch)
        pairs = [ref for part in (*others, *outs) for ref in (x_ref, part)]
        split_kernel(shape, *pairs, *split)

    *part, keep, send = pl.pallas_call(
        kernel,
        grid=(1,),
        out_shape=(*mine, *halves),
        in_specs=[
            pair,
            pl.BlockSpec((rows, lanes), lambda i: (0, key_start)),
            pl.BlockSpec((rows, lanes), lambda i: (0, value_start)),
            pair,
            pl.BlockSpec((1, 4, rows), lambda i: (first, 0, 0)),
            *[whole(array) for array in (begin, cosine, sine, x, *other)],
        ],
        out_specs=[whole(array) for array in (*mine, *halves)],
        scratch_shapes=[
            pltpu.VMEM((rows, rows), F32),
            pltpu.VMEM((2, rows, lanes), F32),
            pltpu.VMEM((2, rows, lanes), F32),
        ],
        compiler_params=pltpu.CompilerParams(vmem_limit_bytes=VMEM_LIMIT),
        cost_estimate=lasting(10.0),
        name="attend_back_last",
    )(qkv, qkv, qkv, grad, lse, begin, cosine, sine, x, *other)
    return part, keep, send


def finish_kernel(parts, *refs):
    across_ref, other_ref, gain_ref = refs[:3]
    weights, outs = refs[3:6], refs[6:10]
    router_out, gain_one_out, gain_two_out, rows_ref, small_ref = refs[10:]
    chip, core = lax.axis_index("expert") // 2, lax.axis_index("expert") % 2
    rows = across_ref.shape[1]
    for m in range(across_ref.shape[0]):
        for ref, own in ((across_ref, core), (other_ref, 1 - core)):
            at = pl.multiple_of((chip ^ m) * 2 * rows + own * rows, rows)
            rows_ref[pl.ds(at, rows), :] = ref[m]
    start = 0
    filled = [0] * 5
    for which, width in parts:
        out, at = (*outs, small_ref)[which], filled[which]
        out[:, at : at + width] = rows_ref[:, start : start + width].astype(F32)
        filled[which] += width
        start += width
    total = None
    for weight, grad in zip(weights, outs):
        part = jnp.sum(weight[...].astype(F32) * grad[...], axis=-1, keepdims=True)
        total = part if total is None else total + part
    height = rows_ref.shape[0]
    same = lax.broadcasted_iota(jnp.int32, (height, height), 0) == lax.broadcasted_iota(
        jnp.int32, (height, height), 1
    )
    experts = router_out.shape[1]
    router_out[...] = small_ref[:, :experts]
    row = jnp.sum(jnp.where(same, total, 0.0), axis=0, keepdims=True)
    gain_one_out[...] = row / gain_ref[...].astype(F32)
    gain_two_out[...] = jnp.sum(
        jnp.where(same, small_ref[:, experts : experts + 1], 0.0), axis=0, keepdims=True
    )


def finish_grads(across, other, parts, experts, weights, gain):
    rows = across.shape[0] * 2 * across.shape[1]
    widths = [sum(w for which, w in parts if which == i) for i in range(5)]
    vmem = pl.BlockSpec(memory_space=pltpu.VMEM)
    shapes = [(rows, width) for width in (*widths[:4], experts)] + [(1, rows)] * 2
    return pl.pallas_call(
        lambda *refs: finish_kernel(parts, *refs),
        out_shape=[jax.ShapeDtypeStruct(shape, F32) for shape in shapes],
        in_specs=[vmem] * 6,
        out_specs=[vmem] * 7,
        scratch_shapes=[
            pltpu.VMEM((rows, across.shape[2]), BF16),
            pltpu.VMEM((rows, widths[4]), F32),
        ],
        compiler_params=pltpu.CompilerParams(vmem_limit_bytes=VMEM_LIMIT),
        cost_estimate=lasting(4.0),
        name="finish_grads",
    )(across, other, gain, *weights)


def local(
    tokens,
    lengths,
    routes,
    cotangent,
    gain_attn,
    w_query,
    key_projection_weight,
    value_projection_weight,
    w_out,
    gain_moe,
    w_router,
    w_gate,
    w_up,
    w_down,
):
    count_of_rows, model_width = tokens.shape
    expert_count = lax.axis_size("expert")
    devices = lax.axis_size("dp")
    e_index = lax.axis_index("expert")
    top_count = routes.shape[1]
    capacity = 2 * count_of_rows * top_count // expert_count
    shard_rows = gain_attn.shape[0]
    query_width = w_query.shape[1]
    key_width = key_projection_weight.shape[1]

    lanes = -(-(expert_count + 2) // 128) * 128
    small = jnp.concatenate(
        [
            w_router,
            gain_attn[:, None],
            gain_moe[:, None],
            jnp.zeros((shard_rows, lanes - expert_count - 2), BF16),
        ],
        axis=1,
    )
    routes_rel = gather_small(routes.T)
    (qkv_w, out_w, small_w), cot_blocks, _ = gather_weights(
        [w_query, key_projection_weight, value_projection_weight, w_out, small],
        (query_width + 2 * key_width, model_width, lanes),
        cotangent,
    )
    router_w = small_w[:, :expert_count]
    gains = small_w[:, expert_count : expert_count + 2].astype(F32).T
    gain_first, gain_second = gains[0], gains[1]

    index_rows = jnp.arange(count_of_rows, dtype=jnp.int32)
    before = (index_rows[:, None] < index_rows[None, :]).astype(BF16)

    def slots_of(expert):
        hit = jnp.any(routes_rel == expert, axis=1)
        place = jnp.dot(hit.astype(BF16), before, preferred_element_type=F32)
        return jnp.where(hit, place.astype(jnp.int32), -1)

    slots_mine = slots_of(e_index)
    slots_sibling = slots_of(e_index ^ 1)
    mine_row = (jnp.arange(lanes) == e_index).astype(F32)[None]
    gate_up_w = jnp.concatenate([w_gate[0], w_up[0]], axis=1)
    down_w = w_down[0]

    _, position = positions_of(lengths[0], count_of_rows)
    begin = (index_rows - position)[None]
    half = HEAD_DIMENSION // 2
    cosine, sine = rope_tables(position, HEAD_DIMENSION)
    cosine = jnp.concatenate([cosine] * 4, axis=1)
    sine = jnp.concatenate([-sine, sine] * 2, axis=1)

    qkv, first_normalized = project(
        tokens, gain_first[None], qkv_w, cosine, sine, query_width, key_width
    )
    attn_rows, lse = attend(qkv, begin, query_width, key_width)
    resid_in = tokens.astype(F32)
    resid_mid = resid_in + jnp.dot(attn_rows, out_w, preferred_element_type=F32)
    inverse_two = lax.rsqrt(jnp.mean(resid_mid * resid_mid, axis=-1, keepdims=True) + eps_norm)
    normed_two = (resid_mid * inverse_two * gain_second).astype(BF16)

    cot_list = [cot_blocks[m] for m in range(expert_count)]
    tok_blocks = {}

    logits = jnp.dot(normed_two, router_w, preferred_element_type=F32)
    expert_ids = jnp.arange(expert_count, dtype=jnp.int32)
    chosen = (routes[:, :, None] == expert_ids[None, None, :]).astype(F32)
    picked = jnp.sum(logits[:, None, :] * chosen, axis=-1)
    gates = jax.nn.softmax(picked, axis=-1)

    even = list(range(0, expert_count, 2))
    groups = [[0], [2, 4], [6]] if expert_count == 8 else [[m] for m in even]
    last_mask = even[-1]
    moe_rows_of, in_rows_of, saved, in_partial = {}, {}, [], {}
    slots_of_pair = {m: jnp.stack([slots_mine[m], slots_sibling[m]]) for m in even}

    def run_group(group):
        masks = [m for low_mask in group for m in (low_mask, low_mask ^ 1)]
        start = masks[0]
        results = expert_group(
            [tok_blocks[m] for m in masks],
            [cot_blocks[m] for m in masks],
            slots_mine[start : start + len(masks)],
            routes_rel[start : start + len(masks)],
            mine_row,
            small_w,
            gate_up_w,
            down_w,
            capacity,
        )
        for i, m in enumerate(masks):
            moe_rows_of[m] = results[i]
            in_rows_of[m] = results[len(masks) + i]
        saved.append(list(results[2 * len(masks) :]))

    def return_rows(group, *earlier):
        rows = []
        for m in group:
            arrived = hop(in_rows_of[m ^ 1], "expert", 1)
            keep = in_rows_of[m]
            rows += [after(keep, *earlier) if earlier else keep, arrived]
        in_partial.update(zip(group, combine(rows, [slots_of_pair[m] for m in group])))

    sent = after(normed_two, slots_mine, slots_sibling, *cot_list)
    tok_blocks[0] = sent
    tok_blocks[1] = hop(sent, "expert", 1)
    run_group([0])
    tok_blocks.update(gather_links(sent, lambda pair: after_all(pair, in_rows_of[0])))
    for m in even[1:]:
        tok_blocks[m ^ 1] = hop(tok_blocks[m], "expert", 1)
    direct = None
    for group in groups[1:]:
        if expert_count == 8:
            earlier = [in_rows_of[1]]
            if group == [last_mask]:
                return_rows([2, 4])
                direct_rows = return_direct(in_partial)
                direct = mixed_hop(direct_rows, 2, 4)
                earlier.append(direct_rows)
            tok_blocks[group[0]] = after(tok_blocks[group[0]], *earlier)
        run_group(group)
    if direct is None:
        for low_mask in even:
            return_rows([low_mask])
    else:
        return_rows([last_mask], direct)
        return_rows([0], in_partial[last_mask])
    saved[0][0] = after(saved[0][0], in_partial[last_mask])
    expert_grads = expert_wgrad(*[list(part) for part in zip(*saved)])
    if direct is None:
        grad_terms = return_halving(in_partial)
        passed = grad_terms[0]
    else:
        passed = after(return_passed(in_partial), expert_grads)
        onward = return_onward(in_partial, passed)
        grad_terms = [in_partial[0], direct, mixed_hop(onward, 4, 2)]
    expert_pieces = lax.psum_scatter(
        after(expert_grads, passed).reshape(-1, model_width), "dp", scatter_dimension=0, tiled=True
    )

    moe_rows = []
    for m in even:
        moe_rows += [moe_rows_of[m], hop(after(moe_rows_of[m ^ 1], passed), "expert", 1)]
    moe_slots = [slots_of_pair[m] for m in even]
    if expert_count == 8:
        moe_list = combine(moe_rows, moe_slots)
        grad_terms = after_all(grad_terms, *moe_list)
    else:
        moe_list = [
            combine(moe_rows[2 * i : 2 * i + 2], moe_slots[i : i + 1])[0]
            for i in range(len(moe_slots))
        ]
    moe_partial = dict(zip(even, moe_list))

    grad_final = cotangent.astype(F32)
    returned = sum_terms(grad_terms)
    gate_columns = returned[:, model_width : model_width + expert_count]
    gate_columns += returned[:, model_width + lanes // 2 :][:, :expert_count]
    grad_gates = jnp.sum(gate_columns[:, None, :] * chosen, axis=-1)
    grad_picked = gates * (grad_gates - jnp.sum(gates * grad_gates, axis=-1, keepdims=True))
    grad_logits = jnp.sum(grad_picked[:, :, None] * chosen, axis=1).astype(BF16)
    grad_normed_two = jnp.dot(grad_logits, router_w.T, preferred_element_type=F32)
    grad_normed_two = grad_normed_two + returned[:, :model_width]
    scaled_two = grad_normed_two * gain_second
    gain_terms = (grad_normed_two * resid_mid * inverse_two).astype(BF16)
    grad_mid = (
        grad_final
        + inverse_two * scaled_two
        - resid_mid
        * inverse_two
        * inverse_two
        * inverse_two
        * jnp.mean(resid_mid * scaled_two, axis=-1, keepdims=True)
    )
    grad_mid_low = grad_mid.astype(BF16)
    grad_attn = lax.dot_general(grad_mid_low, out_w, NT, preferred_element_type=F32).astype(BF16)

    pairs = key_width // (2 * HEAD_DIMENSION)
    cut = pairs // 2
    def back(grad, first, count):
        return attend_back(
            qkv, grad, lse, begin, cosine, sine, query_width, key_width, first, count
        )

    parts = [back(grad_attn, 0, cut)]
    if direct is None:
        moe_terms = return_halving(moe_partial)
        moe_first, moe_last = moe_terms, moe_terms[0]
    else:
        for m in (2, 4, 6):
            moe_partial[m] = after(moe_partial[m], grad_terms[-1])
        moe_first = return_onward(
            moe_partial, after(return_passed(moe_partial), parts[0][0])
        )
        direct_rows = after(return_direct(moe_partial), parts[0][0])
        moe_last = mixed_hop(moe_first, 4, 2)
        moe_terms = [
            moe_partial[0],
            mixed_hop(after(direct_rows, moe_last), 2, 4),
            moe_last,
        ]
        moe_first = (moe_first, direct_rows)
    logits_wide = jnp.pad(grad_logits, ((0, 0), (0, lanes - expert_count)))
    gain_column = jnp.broadcast_to(jnp.arange(lanes) == expert_count, logits_wide.shape)
    early_columns = [[(first_normalized, after(part, *moe_first))] for part in parts[0]]
    early_columns += [
        [(attn_rows, grad_mid_low)],
        [(normed_two, logits_wide), (gain_terms, gain_column.astype(BF16))],
    ]
    fast = model_width % (16 * devices * expert_count) == 0 and pairs == cut + 2
    if fast:
        early_keep, early_send = split_grads(early_columns)
        parts.append(back(after(grad_attn, early_send, moe_last), cut, 1))
        early_near = across_cores(
            early_keep,
            after(early_send, moe_last),
            lambda values: after(values, parts[1][0]),
        )
        part, late_keep, late_send = attend_back_last(
            qkv,
            after(grad_attn, early_near, moe_terms[1]),
            lse,
            begin,
            cosine,
            sine,
            query_width,
            key_width,
            cut + 1,
            first_normalized,
            parts[1],
        )
        parts.append(part)
        line_start, line_far = across_links_start(
            early_near, lambda pieces: after_all(pieces, late_send, expert_pieces)
        )
        late_arrival = hop(after(late_send, line_start), "expert", 1)
    else:
        parts.append(back(grad_attn, cut, pairs - cut))
        line_start = late_send = parts[1][0]
    resid_late, *moe_terms = after_all([resid_mid, *moe_terms], late_send)
    mixed_out = (resid_late + sum_terms(moe_terms)).astype(BF16)
    grad_qkv = jnp.concatenate(
        [after(part[i], line_start) for i in range(3) for part in parts], axis=1
    )
    grad_normed_one = lax.dot_general(grad_qkv, qkv_w, NT, preferred_element_type=F32)
    inverse_one = lax.rsqrt(jnp.mean(resid_in * resid_in, axis=-1, keepdims=True) + eps_norm)
    scaled_one = grad_normed_one * gain_first
    grad_input = (
        grad_mid
        + inverse_one * scaled_one
        - resid_in
        * inverse_one
        * inverse_one
        * inverse_one
        * jnp.mean(resid_in * scaled_one, axis=-1, keepdims=True)
    )
    gate_rows = model_width // devices
    hidden = down_w.shape[0]
    grad_input = grad_input.astype(BF16)
    expert_outs = [
        expert_pieces[None, :gate_rows, :hidden].astype(F32),
        expert_pieces[None, :gate_rows, hidden:].astype(F32),
        expert_pieces[None, gate_rows:, :].astype(F32),
    ]
    projections = (w_query, key_projection_weight, value_projection_weight)
    if fast:
        *line_far, late_arrival = after_all([*line_far, late_arrival], grad_input)
        late_near = join_cores(late_keep, late_arrival)
        late_line = across_links(late_near)
        early_line = (line_start + sum_terms(line_far)).astype(BF16)
        done = across_dp(
            jnp.concatenate([early_line, late_line], axis=-1),
            lambda pieces: after_all(pieces, mixed_out, *expert_outs),
        )
        across = jnp.stack([done] + [hop(done, "expert", m) for m in range(2, expert_count, 2)])
        names = [0, 1, 2, 3, 4] + [0, 1, 2] * 2
        sizes = [part.shape[1] for part in parts[0]] + [model_width, lanes]
        sizes += [part.shape[1] for later in parts[1:] for part in later]
        *columns, grad_out_part, grad_router_part, grad_gain_one, grad_gain_two = finish_grads(
            across,
            hop(across, "expert", 1),
            tuple(zip(names, sizes)),
            expert_count,
            projections,
            gain_attn[None],
        )
        grad_gain_one, grad_gain_two = grad_gain_one[0], grad_gain_two[0]
    else:
        products = [
            sum(lax.dot_general(a, d, TN, preferred_element_type=F32) for a, d in terms)
            for terms in early_columns + [[(first_normalized, part)] for part in parts[1]]
        ]
        total = jnp.concatenate(products, axis=1).astype(BF16)
        total = lax.psum_scatter(total, "dp", scatter_dimension=0, tiled=True)
        total = lax.psum(total, "expert").astype(F32)
        starts = [0]
        for product in products:
            starts.append(starts[-1] + product.shape[1])
        pieces = [total[:, a:d] for a, d in zip(starts, starts[1:])]
        columns = [jnp.concatenate([pieces[i], pieces[5 + i]], axis=1) for i in range(3)]
        grad_out_part, small_part = pieces[3:5]
        grad_router_part, grad_gain_two = small_part[:, :expert_count], small_part[:, expert_count]
        grad_gain_one = sum(
            jnp.sum(weight.astype(F32) * grad, axis=1)
            for weight, grad in zip(projections, columns)
        ) / gain_attn.astype(F32)
    return (
        mixed_out,
        grad_input,
        grad_gain_one,
        *columns,
        grad_out_part,
        grad_gain_two,
        grad_router_part,
        *expert_outs,
    )


def solution(mesh):
    placed = (
        P(("dp", "expert"), None),
        P(("dp", "expert"), None),
        P(("dp", "expert"), None),
        P(("dp", "expert"), None),
        P("dp"),
        P("dp", None),
        P("dp", None),
        P("dp", None),
        P("dp", None),
        P("dp"),
        P("dp", None),
        P("expert", None, None),
        P("expert", None, None),
        P("expert", None, None),
    )
    return jax.shard_map(
        local,
        mesh=mesh,
        in_specs=placed,
        out_specs=(
            P(("dp", "expert"), None),
            P(("dp", "expert"), None),
            P("dp"),
            P("dp", None),
            P("dp", None),
            P("dp", None),
            P("dp", None),
            P("dp"),
            P("dp", None),
            P("expert", "dp", None),
            P("expert", "dp", None),
            P("expert", "dp", None),
        ),
        check_vma=False,
    )
```
